256 devices in a mesh: blk: 16 (over x, y_hi, core), feat: 16 (over y_lo, z).
Axes of the slice: x: 4, y: 4 (y_hi: 2, y_lo: 2; y = y_hi * 2 + y_lo), z: 8, core: 2. Of those that a mesh axis runs over, the one named last changes fastest.
Arguments:
- noise_latents: bfloat16 [16384, 1024], P(('blk', 'feat')), may hold values from -30 to 30, as said below
- data_latents: bfloat16 [16384, 1024], P(('blk', 'feat')), may hold values from -30 to 30, as said below
Outputs:
- velocity: bfloat16 [16384, 1024], P(('blk', 'feat'))
The draws below stay inside these ranges and needn't reach their ends.
Inputs may be any that keep to these rules, and one draw needn't show every extreme that they name: `noise_latents`: pooled latent features. `data_latents`: pooled latent features.
All inputs are finite; a program needn't handle non-finite values.
Results may differ from the reference program's by a relative error of at most 0.013.
Values may be sent and summed in bfloat16 or wider, within the bound.
No kernel may reach another device: no remote copies, remote signals or barrier semaphores. Data moves between devices by JAX's collectives and lax.ppermute only.
A program may use at most 64 MiB of HBM per device.

```python
import math
import jax
import jax.numpy as jnp
from jax import lax

WIDTH = 1024
ROWS_DEV = 1024
ITERS = 3
BATCH = 16384
N_BLK = 16


def latent_rows(key, spread):
    base_rows = jax.random.truncated_normal(key, -6.0, 6.0, (BATCH, WIDTH), jnp.float32)
    subkeys = jax.random.split(jax.random.fold_in(key, 11), 2)
    row_ids = jnp.arange(BATCH)[:, None]
    jitter = jax.random.truncated_normal(subkeys[0], -6.0, 6.0, (BATCH, WIDTH), jnp.float32)
    twin_rows = jitter
    mixed = jnp.where(row_ids % 64 == 1, twin_rows, base_rows)
    pair_scale = jnp.exp(spread * jax.random.uniform(subkeys[1], (BATCH // 2, 1), jnp.float32, -1.0, 1.0))
    row_scale = jnp.repeat(pair_scale, 2, axis=0)
    return row_scale * mixed


def draw_data_latents(key, part):
    values = latent_rows(key, 0.0)
    return values.astype(jnp.bfloat16)


def draw_noise_latents(key, part):
    own_key = jax.random.fold_in(key, 3)
    fresh = jax.random.truncated_normal(own_key, -6.0, 6.0, (BATCH, WIDTH), jnp.float32)
    values = fresh
    return values.astype(jnp.bfloat16)


def setup_inputs(seed: int = 0) -> dict:
    streams_of = jax.random.split(jax.random.key(seed), 3)
    noise_latents = draw_noise_latents(jax.random.fold_in(streams_of[2], 71), 0)
    data_latents = draw_data_latents(jax.random.fold_in(streams_of[2], 71), 0)
    return dict(noise_latents=noise_latents, data_latents=data_latents)


eps_factor = 0.3

def log_sum_exp(values):
    largest = lax.optimization_barrier(jnp.max(values, axis=-1))
    return largest + jnp.log(lax.optimization_barrier(jnp.sum(jnp.exp(values - largest[..., None]), axis=-1)))

def reference(noise_latents, data_latents):
    epsilon = eps_factor * math.sqrt(WIDTH)
    log_mass = -math.log(BATCH)
    data_norms = lax.optimization_barrier(jnp.sum(jnp.square(data_latents.astype(jnp.float32)), axis=1))
    noise_blocks = noise_latents.reshape(N_BLK, ROWS_DEV, WIDTH)

    def distances(noise_block):
        noise_norms = lax.optimization_barrier(jnp.sum(jnp.square(noise_block.astype(jnp.float32)), axis=1))
        products = jnp.dot(noise_block, data_latents.T, preferred_element_type=jnp.float32)
        return noise_norms[:, None] + data_norms[None, :] - 2.0 * products
    cost = lax.map(distances, noise_blocks)
    column_dual = jnp.zeros((BATCH,), jnp.float32)
    for iteration in range(ITERS):

        def row_update(cost_block, column_dual=column_dual):
            return epsilon * log_mass - epsilon * log_sum_exp((column_dual[None, :] - cost_block) / epsilon)
        row_dual = lax.map(row_update, cost)

        def column_step(running, blocks):
            run_max, run_sum = running
            cost_block, row_block = blocks
            scores = (row_block[:, None] - cost_block) / epsilon
            new_max = jnp.maximum(run_max, lax.optimization_barrier(jnp.max(scores, axis=0)))
            new_sum = run_sum * jnp.exp(run_max - new_max) + lax.optimization_barrier(jnp.sum(jnp.exp(scores - new_max[None, :]), axis=0))
            return ((new_max, new_sum), None)
        start_state = (jnp.full((BATCH,), -jnp.inf, jnp.float32), jnp.zeros((BATCH,), jnp.float32))
        (column_max, column_total), unused = lax.scan(column_step, start_state, (cost, row_dual))
        column_dual = epsilon * log_mass - epsilon * (column_max + jnp.log(column_total))

    def targets(blocks):
        cost_block, noise_block = blocks
        scores = (column_dual[None, :] - cost_block) / epsilon
        row_top = lax.optimization_barrier(jnp.max(scores, axis=1))
        exps = jnp.exp(scores - row_top[:, None])
        row_total = lax.optimization_barrier(jnp.sum(exps, axis=1))
        weights = exps.astype(jnp.bfloat16)
        target = jnp.dot(weights, data_latents, preferred_element_type=jnp.float32) / row_total[:, None]
        return (target - noise_block.astype(jnp.float32)).astype(jnp.bfloat16)
    result_rows = lax.map(targets, (cost, noise_blocks))
    return result_rows.reshape(BATCH, WIDTH)
```

```python
import math

import jax
import jax.numpy as jnp
from jax import lax
from jax.sharding import Mesh
from jax.sharding import PartitionSpec as P

WIDTH = 1024
eps_factor = 0.3

AXES = ("x", "yh", "core", "yl", "z")
SIZES = (4, 2, 2, 2, 8)
ROW_GROUP = ("core", "z")
COL_GROUP = ("x", "yh", "yl")


def device_pairs(move):
    pairs = []
    for x in range(4):
        for yh in range(2):
            for core in range(2):
                for yl in range(2):
                    for z in range(8):
                        place = (x, yh, core, yl, z)
                        pairs.append((number(place), number(move(*place))))
    return pairs


def number(place):
    index = 0
    for size, at in zip(SIZES, place):
        index = index * size + at % size
    return index


def shift_z(a, by):
    return lax.ppermute(a, AXES, device_pairs(lambda x, yh, c, yl, z: (x, yh, c, yl, z + by)))


def swap_core(a):
    return lax.ppermute(a, AXES, device_pairs(lambda x, yh, c, yl, z: (x, yh, 1 - c, yl, z)))


def spread(vector, group):
    wide = vector.reshape(1, 8, 128)
    copies = jnp.broadcast_to(wide, (16, 8, 128))
    return lax.all_to_all(copies, group, 0, 0).reshape(16, vector.shape[0])


def log_sum_exp(values, axis):
    top = jnp.max(values, axis=axis)
    total = jnp.sum(jnp.exp(values - jnp.expand_dims(top, axis)), axis=axis)
    return top + jnp.log(total)


def per_device(noise_latents, data_latents):
    piece = noise_latents.shape[0]
    batch = piece * 256
    epsilon = eps_factor * math.sqrt(WIDTH)
    log_mass = -math.log(batch)
    core = lax.axis_index("core")

    along_z = lax.all_gather(noise_latents, "z", axis=0, tiled=True)
    other = swap_core(along_z)
    first = jnp.where(core == 0, along_z, other)
    second = jnp.where(core == 0, other, along_z)
    noise_full = jnp.concatenate([first, second], axis=0)
    columns = lax.all_to_all(
        jnp.broadcast_to(data_latents[None], (16,) + data_latents.shape), COL_GROUP, 0, 0
    ).reshape(16 * piece, WIDTH)

    noise_norms = jnp.sum(jnp.square(noise_full.astype(jnp.float32)), axis=1)
    data_norms = jnp.sum(jnp.square(columns.astype(jnp.float32)), axis=1)
    products = lax.dot_general(
        noise_full, columns, (((1,), (1,)), ((), ())), preferred_element_type=jnp.float32
    )
    cost = noise_norms[:, None] + data_norms[None, :] - 2.0 * products

    row_lse = log_sum_exp(spread(log_sum_exp(-cost / epsilon, 1), ROW_GROUP), 0)
    row_dual = epsilon * log_mass - epsilon * row_lse
    col_lse = log_sum_exp(
        spread(log_sum_exp((row_dual[:, None] - cost) / epsilon, 0), COL_GROUP), 0
    )
    column_dual = epsilon * log_mass - epsilon * col_lse

    plan = jnp.exp((row_dual[:, None] + column_dual[None, :] - cost) / epsilon - log_mass)
    scale = None
    for iteration in range(2):
        scaled = plan if scale is None else plan * scale[None, :]
        row_sum = jnp.sum(spread(jnp.sum(scaled, axis=1), ROW_GROUP), axis=0)
        col_sum = jnp.sum(spread(jnp.sum(plan / row_sum[:, None], axis=0), COL_GROUP), axis=0)
        scale = 1.0 / col_sum
    scaled = plan * scale[None, :]
    totals = jnp.sum(scaled, axis=1)
    weights = scaled.astype(jnp.bfloat16)
    partial = jnp.dot(weights, columns, preferred_element_type=jnp.float32)

    high = totals.astype(jnp.bfloat16)
    low = (totals - high.astype(jnp.float32)).astype(jnp.bfloat16)
    tail = jnp.concatenate(
        [jnp.broadcast_to(high[:, None], (1024, 64)), jnp.broadcast_to(low[:, None], (1024, 64))], 1
    )
    halves = partial.astype(jnp.bfloat16).reshape(2, 8, piece, WIDTH)
    tails = tail.reshape(2, 8, piece, 128)

    def with_tail(a, b):
        return jnp.concatenate([a, b], axis=-1)

    def half(which):
        return with_tail(
            lax.dynamic_index_in_dim(halves, which, 0, False),
            lax.dynamic_index_in_dim(tails, which, 0, False),
        )

    def add(a, b):
        a32, b32 = a.astype(jnp.float32), b.astype(jnp.float32)
        body = a32[..., :WIDTH] + b32[..., :WIDTH]
        mass = a32[..., WIDTH : WIDTH + 64] + a32[..., WIDTH + 64 :]
        mass = mass + b32[..., WIDTH : WIDTH + 64] + b32[..., WIDTH + 64 :]
        return body, mass

    def packed(body, mass):
        upper = mass.astype(jnp.bfloat16)
        lower = (mass - upper.astype(jnp.float32)).astype(jnp.bfloat16)
        return jnp.concatenate([body.astype(jnp.bfloat16), upper, lower], axis=-1)

    own_half = packed(*add(half(core), swap_core(half(1 - core))))
    z = lax.axis_index("z")

    def own(offset):
        return lax.dynamic_index_in_dim(own_half, (z + offset) % 8, 0, False)

    right, left = own(4), own(5)
    right = shift_z(right, 1)
    for k in (3, 2, 1):
        right, left = (
            shift_z(packed(*add(right, own(k))), 1),
            shift_z(left if k == 3 else packed(*add(left, own(8 - k))), -1),
        )
    body, mass = add(right, left)
    body = body + own(0)[..., :WIDTH].astype(jnp.float32)
    mass = mass + own(0)[..., WIDTH : WIDTH + 64].astype(jnp.float32)
    mass = mass + own(0)[..., WIDTH + 64 :].astype(jnp.float32)
    target = body / mass[:, :1]
    return (target - noise_latents.astype(jnp.float32)).astype(jnp.bfloat16)


def solution(mesh):
    fine = Mesh(mesh.devices.reshape(SIZES), AXES)
    rows = P(AXES, None)
    return jax.shard_map(
        per_device, mesh=fine, in_specs=(rows, rows), out_specs=rows, check_vma=False
    )
```

```python
import math

import jax
import jax.numpy as jnp
from jax import lax
from jax.sharding import Mesh
from jax.sharding import PartitionSpec as P

WIDTH = 1024
eps_factor = 0.3

AXES = ("x", "yh", "core", "yl", "z")
SIZES = (4, 2, 2, 2, 8)
ROW_GROUP = ("core", "z")
COL_GROUP = ("x", "yh", "yl")


def device_pairs(move):
    pairs = []
    for x in range(4):
        for yh in range(2):
            for core in range(2):
                for yl in range(2):
                    for z in range(8):
                        place = (x, yh, core, yl, z)
                        pairs.append((number(place), number(move(*place))))
    return pairs


def number(place):
    index = 0
    for size, at in zip(SIZES, place):
        index = index * size + at % size
    return index


def shift_z(a, by):
    return lax.ppermute(a, AXES, device_pairs(lambda x, yh, c, yl, z: (x, yh, c, yl, z + by)))


def swap_core(a):
    return lax.ppermute(a, AXES, device_pairs(lambda x, yh, c, yl, z: (x, yh, 1 - c, yl, z)))


def spread(vector, group):
    wide = vector.reshape(1, 8, 128)
    copies = jnp.broadcast_to(wide, (16, 8, 128))
    return lax.all_to_all(copies, group, 0, 0).reshape(16, vector.shape[0])


def log_sum_exp(values, axis):
    top = jnp.max(values, axis=axis)
    total = jnp.sum(jnp.exp(values - jnp.expand_dims(top, axis)), axis=axis)
    return top + jnp.log(total)


def put(whole, part, at):
    return lax.dynamic_update_index_in_dim(whole, part, at, 0)


def pick(whole, at):
    return lax.dynamic_index_in_dim(whole, at, 0, False)


def added(a, b):
    return (a.astype(jnp.float32) + b.astype(jnp.float32)).astype(jnp.bfloat16)


def gather_z(part):
    z = lax.axis_index("z")
    whole = put(jnp.zeros((8,) + part.shape, part.dtype), part, z)
    right = left = part
    for k in (1, 2, 3, 4):
        right = shift_z(right, 1)
        whole = put(whole, right, jnp.bitwise_and(z - k, 7))
        if k < 4:
            left = shift_z(left, -1)
            whole = put(whole, left, jnp.bitwise_and(z + k, 7))
    return whole


def scatter_z(parts):
    z = lax.axis_index("z")

    def own(offset):
        return pick(parts, jnp.bitwise_and(z + offset, 7))

    right, left = shift_z(own(4), 1), shift_z(own(5), -1)
    for k in (3, 2, 1):
        right = shift_z(added(right, own(k)), 1)
        if k > 1:
            left = shift_z(added(left, own(9 - k)), -1)
    last = [a.astype(jnp.float32) for a in (right, left, own(0))]
    return last[0] + last[1] + last[2]


def per_device(noise_latents, data_latents):
    piece = noise_latents.shape[0]
    batch = piece * 256
    epsilon = eps_factor * math.sqrt(WIDTH)
    log_mass = -math.log(batch)
    core = lax.axis_index("core")

    columns = lax.all_to_all(
        jnp.broadcast_to(data_latents[None], (16,) + data_latents.shape), COL_GROUP, 0, 0
    ).reshape(16 * piece, WIDTH)
    along_z = gather_z(noise_latents)
    both = put(jnp.zeros((2,) + along_z.shape, along_z.dtype), along_z, core)
    noise_full = put(both, swap_core(along_z), 1 - core).reshape(16 * piece, WIDTH)

    noise_norms = jnp.sum(jnp.square(noise_full.astype(jnp.float32)), axis=1)
    data_norms = jnp.sum(jnp.square(columns.astype(jnp.float32)), axis=1)
    products = lax.dot_general(
        noise_full, columns, (((1,), (1,)), ((), ())), preferred_element_type=jnp.float32
    )
    cost = noise_norms[:, None] + data_norms[None, :] - 2.0 * products

    row_lse = log_sum_exp(spread(log_sum_exp(-cost / epsilon, 1), ROW_GROUP), 0)
    row_dual = epsilon * log_mass - epsilon * row_lse
    col_lse = log_sum_exp(
        spread(log_sum_exp((row_dual[:, None] - cost) / epsilon, 0), COL_GROUP), 0
    )
    column_dual = epsilon * log_mass - epsilon * col_lse

    plan = lax.optimization_barrier(
        jnp.exp((row_dual[:, None] + column_dual[None, :] - cost) / epsilon - log_mass)
    )
    row_sum = jnp.sum(spread(jnp.sum(plan, axis=1), ROW_GROUP), axis=0)
    col_sum = jnp.sum(spread(jnp.sum(plan * (1.0 / row_sum)[:, None], axis=0), COL_GROUP), axis=0)
    row_sum = jnp.sum(spread(jnp.sum(plan * (1.0 / col_sum)[None, :], axis=1), ROW_GROUP), axis=0)
    col_sum = jnp.sum(spread(jnp.sum(plan * (1.0 / row_sum)[:, None], axis=0), COL_GROUP), axis=0)

    scaled = plan * (1.0 / col_sum)[None, :]
    weights = scaled.astype(jnp.bfloat16)
    row_total = jnp.sum(spread(jnp.sum(scaled, axis=1), ROW_GROUP), axis=0)
    partial = jnp.dot(weights, columns, preferred_element_type=jnp.float32)
    halves = partial.astype(jnp.bfloat16).reshape(2, 8, piece, WIDTH)

    own_half = added(pick(halves, core), swap_core(pick(halves, 1 - core)))
    summed_up = scatter_z(own_half)
    z = lax.axis_index("z")
    own_total = lax.dynamic_slice_in_dim(row_total, (core * 8 + z) * piece, piece, 0)
    target = summed_up / own_total[:, None]
    return (target - noise_latents.astype(jnp.float32)).astype(jnp.bfloat16)


def solution(mesh):
    fine = Mesh(mesh.devices.reshape(SIZES), AXES)
    rows = P(AXES, None)
    return jax.shard_map(
        per_device, mesh=fine, in_specs=(rows, rows), out_specs=rows, check_vma=False
    )
```

```python
import functools
import math

import jax
import jax.numpy as jnp
from jax import lax
from jax.experimental import pallas as pl
from jax.experimental.pallas import tpu as pltpu
from jax.sharding import Mesh
from jax.sharding import PartitionSpec as P

WIDTH = 1024
ROWS = 1024
eps_factor = 0.3

AXES = ("x", "yh", "core", "yl", "z")
SIZES = (4, 2, 2, 2, 8)
ROW_GROUP = ("core", "z")
COL_GROUP = ("x", "yh", "yl")

EPSILON = eps_factor * math.sqrt(WIDTH)
LOG2E = math.log2(math.e)
LOG2_MASS = -math.log2(16384)


def device_pairs(move):
    pairs = []
    for x in range(4):
        for yh in range(2):
            for core in range(2):
                for yl in range(2):
                    for z in range(8):
                        place = (x, yh, core, yl, z)
                        pairs.append((number(place), number(move(*place))))
    return pairs


def number(place):
    index = 0
    for size, at in zip(SIZES, place):
        index = index * size + at % size
    return index


def shift_z(a, by):
    return lax.ppermute(a, AXES, device_pairs(lambda x, yh, c, yl, z: (x, yh, c, yl, z + by)))


def swap_core(a):
    return lax.ppermute(a, AXES, device_pairs(lambda x, yh, c, yl, z: (x, yh, 1 - c, yl, z)))


def spread(copies, group):
    return lax.all_to_all(copies, group, 0, 0)


def put(whole, part, at):
    return lax.dynamic_update_index_in_dim(whole, part, at, 0)


def pick(whole, at):
    return lax.dynamic_index_in_dim(whole, at, 0, False)


def added(a, b):
    return (a.astype(jnp.float32) + b.astype(jnp.float32)).astype(jnp.bfloat16)


def gather_z(part):
    z = lax.axis_index("z")
    whole = put(jnp.zeros((8,) + part.shape, part.dtype), part, z)
    right = left = part
    for k in (1, 2, 3, 4):
        right = shift_z(right, 1)
        whole = put(whole, right, jnp.bitwise_and(z - k, 7))
        if k < 4:
            left = shift_z(left, -1)
            whole = put(whole, left, jnp.bitwise_and(z + k, 7))
    return whole


def scatter_z(parts):
    z = lax.axis_index("z")

    def own(offset):
        return pick(parts, jnp.bitwise_and(z + offset, 7))

    right, left = shift_z(own(4), 1), shift_z(own(5), -1)
    for k in (3, 2, 1):
        right = shift_z(added(right, own(k)), 1)
        if k > 1:
            left = shift_z(added(left, own(9 - k)), -1)
    last = [a.astype(jnp.float32) for a in (right, left, own(0))]
    return last[0] + last[1] + last[2]


def to_lanes(square):
    return jnp.concatenate([square[k : k + 1, :] for k in range(8)], axis=1)


def to_square(lanes):
    return jnp.concatenate([lanes[:, 128 * k : 128 * k + 128] for k in range(8)], axis=0)


def own_first(square):
    swapped = jnp.concatenate([square[4:, :], square[:4, :]], axis=0)
    return jnp.where(lax.axis_index("core") == 0, square, swapped)


def lse2(parts):
    top = jnp.max(parts, axis=0)
    return top + jnp.log2(jnp.sum(jnp.exp2(parts - top[None]), axis=0))


def send(out_ref, square):
    out_ref[...] = jnp.broadcast_to(square[None], (16, 8, 128))


def terms(lanes):
    high = lanes.astype(jnp.bfloat16)
    rest = lanes - high.astype(jnp.float32)
    low = rest.astype(jnp.bfloat16)
    zeros = jnp.zeros((14, ROWS), jnp.bfloat16)
    return jnp.concatenate([high, low, zeros], axis=0)


def down(row):
    return jnp.transpose(jnp.broadcast_to(row, (128, 128)))[:, :1]


def across(column):
    return jnp.transpose(jnp.broadcast_to(column, (128, 128)))[:1, :]


def square_sums(block):
    wide = block.astype(jnp.float32)
    return jnp.sum(wide * wide, axis=1, keepdims=True)


def scores_kernel(data_ref, own_ref, other_ref, score_ref, out_ref):
    scale = LOG2E / EPSILON
    data_norms = jnp.concatenate(
        [square_sums(data_ref[pl.ds(128 * k, 128), :]) for k in range(8)], axis=0
    )
    rows = []
    for k in range(4):
        source = own_ref if k < 2 else other_ref
        noise = source[pl.ds(256 * (k % 2), 256), :]
        noise_norms = jnp.concatenate(
            [across(square_sums(noise[:128])), across(square_sums(noise[128:]))], axis=1
        )
        products = lax.dot_general(
            data_ref[...], noise, (((1,), (1,)), ((), ())), preferred_element_type=jnp.float32
        )
        scores = (2.0 * products - (data_norms + noise_norms)) * scale
        score_ref[:, pl.ds(256 * k, 256)] = scores
        top = jnp.max(scores, axis=0, keepdims=True)
        total = jnp.sum(jnp.exp2(scores - top), axis=0, keepdims=True)
        rows.append(top + jnp.log2(total))
    send(out_ref, own_first(to_square(jnp.concatenate(rows, axis=1))))


def columns_kernel(score_ref, in_ref, dual_ref, out_ref):
    dual = own_first(LOG2_MASS - lse2(in_ref[...]))
    dual_ref[...] = dual
    along = to_lanes(dual)
    rows = []
    for k in range(8):
        shifted = score_ref[pl.ds(128 * k, 128), :] + along
        top = jnp.max(shifted, axis=1, keepdims=True)
        total = jnp.sum(jnp.exp2(shifted - top), axis=1, keepdims=True)
        rows.append(across(top + jnp.log2(total)))
    send(out_ref, jnp.concatenate(rows, axis=0))


def plan_kernel(score_ref, dual_ref, in_ref, plan_ref, out_ref):
    along = to_lanes(dual_ref[...])
    dual = LOG2_MASS - lse2(in_ref[...])
    sums = jnp.zeros((1, ROWS), jnp.float32)
    for k in range(8):
        part = pl.ds(128 * k, 128)
        lifted = down(dual[k : k + 1, :] - LOG2_MASS)
        plan = jnp.exp2(score_ref[part, :] + along + lifted)
        plan_ref[part, :] = plan.astype(jnp.bfloat16)
        sums = sums + jnp.sum(plan, axis=0, keepdims=True)
    send(out_ref, own_first(to_square(sums)))


def column_sums_kernel(plan_ref, in_ref, out_ref):
    scale = own_first(1.0 / jnp.sum(in_ref[...], axis=0))
    sums = lax.dot_general(
        terms(to_lanes(scale)),
        plan_ref[...],
        (((1,), (1,)), ((), ())),
        preferred_element_type=jnp.float32,
    )
    send(out_ref, to_square(sums[0:1, :] + sums[1:2, :]))


def row_sums_kernel(plan_ref, in_ref, out_ref):
    scale = 1.0 / jnp.sum(in_ref[...], axis=0)
    sums = jnp.dot(terms(to_lanes(scale)), plan_ref[...], preferred_element_type=jnp.float32)
    send(out_ref, own_first(to_square(sums[0:1, :] + sums[1:2, :])))


def targets_kernel(plan_ref, in_ref, data_ref, own_ref, other_ref, out_ref, weight_ref):
    scale = 1.0 / jnp.sum(in_ref[...], axis=0)
    sums = jnp.zeros((1, ROWS), jnp.float32)
    for k in range(8):
        part = pl.ds(128 * k, 128)
        weights = plan_ref[part, :].astype(jnp.float32) * down(scale[k : k + 1, :])
        weight_ref[part, :] = weights.astype(jnp.bfloat16)
        sums = sums + jnp.sum(weights, axis=0, keepdims=True)
    send(out_ref, own_first(to_square(sums)))
    for k in range(4):
        partial = lax.dot_general(
            weight_ref[:, pl.ds(256 * k, 256)],
            data_ref[...],
            (((0,), (0,)), ((), ())),
            preferred_element_type=jnp.float32,
        ).astype(jnp.bfloat16)
        home = own_ref if k < 2 else other_ref
        home[pl.ds(256 * (k % 2), 256), :] = partial


SQUARE = jax.ShapeDtypeStruct((8, 128), jnp.float32)
COPIES = jax.ShapeDtypeStruct((16, 8, 128), jnp.float32)


def in_vmem(rows, dtype):
    return pltpu.VMEM((rows, 1024), dtype)


def run(kernel, outs, *args, flops=0, scratch=()):
    return pl.pallas_call(
        kernel,
        out_shape=outs,
        in_specs=[pl.BlockSpec(memory_space=pltpu.VMEM)] * len(args),
        out_specs=jax.tree.map(lambda _: pl.BlockSpec(memory_space=pltpu.VMEM), outs),
        scratch_shapes=scratch,
        compiler_params=pltpu.CompilerParams(vmem_limit_bytes=40 * 1024 * 1024),
        cost_estimate=pl.CostEstimate(flops=flops, bytes_accessed=4 << 20, transcendentals=0),
    )(*args)


def keep(a):
    return pltpu.with_memory_space_constraint(a, pltpu.VMEM)


def per_device(noise_latents, data_latents):
    piece = noise_latents.shape[0]
    core, z = lax.axis_index("core"), lax.axis_index("z")

    columns = spread(
        jnp.broadcast_to(data_latents[None], (16,) + data_latents.shape), COL_GROUP
    ).reshape(ROWS, WIDTH)
    own_rows = gather_z(noise_latents).reshape(ROWS // 2, WIDTH)
    other_rows = swap_core(own_rows)

    scores, parts = run(
        scores_kernel, (in_vmem(ROWS, jnp.float32), COPIES), columns, own_rows, other_rows
    )
    scores = keep(scores)
    row_dual, parts = run(columns_kernel, (SQUARE, COPIES), scores, spread(parts, ROW_GROUP))
    plan, parts = run(
        plan_kernel,
        (in_vmem(ROWS, jnp.bfloat16), COPIES),
        scores,
        row_dual,
        spread(parts, COL_GROUP),
    )
    plan = keep(plan)
    parts = run(column_sums_kernel, COPIES, plan, spread(parts, ROW_GROUP))
    parts = run(row_sums_kernel, COPIES, plan, spread(parts, COL_GROUP))
    parts = run(column_sums_kernel, COPIES, plan, spread(parts, ROW_GROUP))
    half = jax.ShapeDtypeStruct((ROWS // 2, WIDTH), jnp.bfloat16)
    own_half, other_half, parts = run(
        targets_kernel,
        (half, half, COPIES),
        plan,
        spread(parts, COL_GROUP),
        columns,
        scratch=[pltpu.VMEM((ROWS, ROWS), jnp.bfloat16)],
    )
    row_total = jnp.sum(spread(parts, ROW_GROUP), axis=0).reshape(16, piece)

    own_half = added(own_half, swap_core(other_half)).reshape(8, piece, WIDTH)
    summed_up = scatter_z(own_half)
    target = summed_up / pick(row_total, core * 8 + z)[:, None]
    return (target - noise_latents.astype(jnp.float32)).astype(jnp.bfloat16)


def solution(mesh):
    fine = Mesh(mesh.devices.reshape(SIZES), AXES)
    rows = P(AXES, None)
    return jax.shard_map(
        per_device, mesh=fine, in_specs=(rows, rows), out_specs=rows, check_vma=False
    )
```

```python
import functools
import math

import jax
import jax.numpy as jnp
from jax import lax
from jax.experimental import pallas as pl
from jax.experimental.pallas import tpu as pltpu
from jax.sharding import Mesh
from jax.sharding import PartitionSpec as P

WIDTH = 1024
ROWS = 1024
eps_factor = 0.3

AXES = ("x", "yh", "core", "yl", "z")
SIZES = (4, 2, 2, 2, 8)
ROW_GROUP = ("core", "z")
COL_GROUP = ("x", "yh", "yl")

EPSILON = eps_factor * math.sqrt(WIDTH)
LOG2E = math.log2(math.e)
LOG2_MASS = -math.log2(16384)


PIECE = 64
BLOCK = 2 * PIECE
TAIL = 16
FAR = PIECE + TAIL
FULL = BLOCK + TAIL


def number(place):
    index = 0
    for size, at in zip(SIZES, place):
        index = index * size + at % size
    return index


def moved(a, move):
    pairs = []
    for x in range(4):
        for y in range(4):
            for core in range(2):
                for z in range(8):
                    tx, ty, tcore, tz = move(x, y, core, z)
                    source = (x, y // 2, core, y % 2, z)
                    pairs.append((number(source), number((tx, ty // 2, tcore, ty % 2, tz))))
    return lax.ppermute(a, AXES, pairs)


def swap_core(a):
    return moved(a, lambda x, y, core, z: (x, y, 1 - core, z))


def shift_z(a):
    return moved(a, lambda x, y, core, z: (x, y, core, z + 1 - 2 * core))


def swap_x(a, flips):
    return moved(a, lambda x, y, core, z: (x ^ flips[core], y, core, z))


def swap_y(a, flips):
    return moved(a, lambda x, y, core, z: (x, y ^ flips[core], core, z))


def spread(copies, group):
    return lax.all_to_all(copies, group, 0, 0)


def gather_columns(data):
    core, x = lax.axis_index("core"), lax.axis_index("x")
    yh, yl = lax.axis_index("yh"), lax.axis_index("yl")
    x0, x1 = x % 2, x // 2
    along_x = [
        (swap_x, (1, 3), jnp.where(core == 0, x0, x1)),
        (swap_x, (3, 1), jnp.where(core == 0, x1, x0 ^ x1)),
    ]
    along_y = [
        (swap_y, (1, 3), jnp.where(core == 0, yl, yh)),
        (swap_y, (3, 1), jnp.where(core == 0, yh, yl ^ yh)),
    ]
    parts = [data[: PIECE // 2], data[PIECE // 2 :]]
    for step in range(4):
        plans = (along_x + along_y)[step], (along_y + along_x)[step]
        received = [swap(part, flips) for part, (swap, flips, _) in zip(parts, plans)]
        parts = [
            jnp.where(
                at == 0,
                jnp.concatenate([part, other], axis=0),
                jnp.concatenate([other, part], axis=0),
            )
            for part, other, (_, _, at) in zip(parts, received, plans)
        ]
    return parts


def gather_rows(noise):
    beside = swap_core(noise)
    blocks = [jnp.concatenate([noise, beside], axis=0)]
    for step in range(3):
        blocks.append(shift_z(blocks[-1]))
    far = shift_z(blocks[-1][:PIECE])
    others = swap_core(jnp.concatenate(blocks[1:] + [far], axis=0))
    return [noise, beside] + blocks[1:] + [far, others]


def to_lanes(square):
    return jnp.concatenate([square[k : k + 1, :] for k in range(8)], axis=1)


def to_square(lanes):
    return jnp.concatenate([lanes[:, 128 * k : 128 * k + 128] for k in range(8)], axis=0)


def own_first(square):
    swapped = jnp.concatenate([square[:, PIECE:], square[:, :PIECE]], axis=1)
    return jnp.where(lax.axis_index("core") == 0, square, swapped)


def lse2(parts):
    top = jnp.max(parts, axis=0)
    return top + jnp.log2(jnp.sum(jnp.exp2(parts - top[None]), axis=0))


def send(out_ref, square):
    out_ref[...] = jnp.broadcast_to(square[None], (16, 8, 128))


def terms(lanes):
    high = lanes.astype(jnp.bfloat16)
    rest = lanes - high.astype(jnp.float32)
    low = rest.astype(jnp.bfloat16)
    zeros = jnp.zeros((14, ROWS), jnp.bfloat16)
    return jnp.concatenate([high, low, zeros], axis=0)


def down(row):
    return jnp.transpose(jnp.broadcast_to(row, (128, 128)))[:, :1]


def across(column):
    return jnp.transpose(jnp.broadcast_to(column, (128, 128)))[:1, :]


def square_sums(block):
    wide = block.astype(jnp.float32)
    return jnp.sum(wide * wide, axis=1, keepdims=True)


def along_z(steps):
    return jnp.bitwise_and(lax.axis_index("z") + (1 - 2 * lax.axis_index("core")) * steps, 7)


def flipped(block):
    return jnp.concatenate([block[PIECE:], block[:PIECE]], axis=0)


def scores_kernel(
    data0, data1, own, beside, near1, near2, near3, far, others, score_ref, out_ref, lse_ref
):
    scale = LOG2E / EPSILON
    pairs = [
        (0, 4, jnp.concatenate([own[...], beside[...], far[...], others[pl.ds(3 * BLOCK, PIECE), :]], axis=0))
    ]
    for k, near in ((1, near1), (2, near2), (3, near3)):
        other = flipped(others[pl.ds((k - 1) * BLOCK, BLOCK), :])
        pairs.append((-k, k, jnp.concatenate([near[...], other], axis=0)))
    data_norms = [
        jnp.concatenate([square_sums(data[pl.ds(128 * k, 128), :]) for k in range(4)], axis=0)
        for data in (data0, data1)
    ]
    for first, second, noise in pairs:
        noise_norms = jnp.concatenate(
            [across(square_sums(noise[:BLOCK])), across(square_sums(noise[BLOCK:]))], axis=1
        )
        halves = []
        for data, norms in zip((data0, data1), data_norms):
            products = lax.dot_general(
                data[...], noise, (((1,), (1,)), ((), ())), preferred_element_type=jnp.float32
            )
            halves.append((2.0 * products - (norms + noise_norms)) * scale)
        top = jnp.maximum(
            jnp.max(halves[0], axis=0, keepdims=True), jnp.max(halves[1], axis=0, keepdims=True)
        )
        total = jnp.sum(jnp.exp2(halves[0] - top), axis=0, keepdims=True) + jnp.sum(
            jnp.exp2(halves[1] - top), axis=0, keepdims=True
        )
        row = top + jnp.log2(total)
        for side, steps in enumerate((first, second)):
            at = along_z(steps)
            lanes = slice(BLOCK * side, BLOCK * side + BLOCK)
            lse_ref[pl.ds(at, 1), :] = row[:, lanes]
            for h in range(2):
                score_ref[pl.ds(512 * h, 512), pl.ds(pl.multiple_of(at * 128, 128), 128)] = halves[h][:, lanes]
    send(out_ref, own_first(lse_ref[...]))


def columns_kernel(score_ref, in_ref, dual_ref, out_ref):
    dual = own_first(LOG2_MASS - lse2(in_ref[...]))
    dual_ref[...] = dual
    along = to_lanes(dual)
    rows = []
    for k in range(8):
        shifted = score_ref[pl.ds(128 * k, 128), :] + along
        top = jnp.max(shifted, axis=1, keepdims=True)
        total = jnp.sum(jnp.exp2(shifted - top), axis=1, keepdims=True)
        rows.append(across(top + jnp.log2(total)))
    send(out_ref, jnp.concatenate(rows, axis=0))


def plan_kernel(score_ref, dual_ref, in_ref, plan_ref, out_ref):
    along = to_lanes(dual_ref[...])
    dual = LOG2_MASS - lse2(in_ref[...])
    sums = jnp.zeros((1, ROWS), jnp.float32)
    for k in range(8):
        part = pl.ds(128 * k, 128)
        lifted = down(dual[k : k + 1, :] - LOG2_MASS)
        plan = jnp.exp2(score_ref[part, :] + along + lifted)
        plan_ref[part, :] = plan.astype(jnp.bfloat16)
        sums = sums + jnp.sum(plan, axis=0, keepdims=True)
    send(out_ref, own_first(to_square(sums)))


def column_sums_kernel(plan_ref, in_ref, out_ref):
    scale = own_first(1.0 / jnp.sum(in_ref[...], axis=0))
    sums = lax.dot_general(
        terms(to_lanes(scale)),
        plan_ref[...],
        (((1,), (1,)), ((), ())),
        preferred_element_type=jnp.float32,
    )
    send(out_ref, to_square(sums[0:1, :] + sums[1:2, :]))


def row_sums_kernel(plan_ref, in_ref, out_ref):
    scale = 1.0 / jnp.sum(in_ref[...], axis=0)
    sums = jnp.dot(terms(to_lanes(scale)), plan_ref[...], preferred_element_type=jnp.float32)
    send(out_ref, own_first(to_square(sums[0:1, :] + sums[1:2, :])))


def packed(total):
    high = total.astype(jnp.bfloat16)
    low = (total - high.astype(jnp.float32)).astype(jnp.bfloat16)
    zeros = jnp.zeros((TAIL - 2, 128), jnp.bfloat16)
    narrow = jnp.concatenate([high, low, zeros], axis=0)
    return jnp.concatenate([narrow, jnp.zeros((TAIL, WIDTH - 128), jnp.bfloat16)], axis=1)


def unpacked(tail):
    return tail[0:1, :128].astype(jnp.float32) + tail[1:2, :128].astype(jnp.float32)


def halves_turned(total):
    return jnp.concatenate([total[:, PIECE:], total[:, :PIECE]], axis=1)


def targets_kernel(plan_ref, in_ref, data0, data1, mine_ref, give_ref, weight_ref, sum_ref):
    scale = 1.0 / jnp.sum(in_ref[...], axis=0)
    sums = jnp.zeros((1, ROWS), jnp.float32)
    for k in range(8):
        part = pl.ds(128 * k, 128)
        weights = plan_ref[part, :].astype(jnp.float32) * down(scale[k : k + 1, :])
        weight_ref[part, :] = weights.astype(jnp.bfloat16)
        sums = sums + jnp.sum(weights, axis=0, keepdims=True)
    sum_ref[...] = to_square(sums)

    def partial(first, second):
        at = [along_z(first), along_z(second)]
        weights = jnp.concatenate(
            [weight_ref[:, pl.ds(pl.multiple_of(k * 128, 128), 128)] for k in at], axis=1
        )
        out = 0.0
        for h, data in enumerate((data0, data1)):
            out = out + lax.dot_general(
                weights[512 * h : 512 * h + 512],
                data[...],
                (((0,), (0,)), ((), ())),
                preferred_element_type=jnp.float32,
            )
        return out.astype(jnp.bfloat16), [sum_ref[pl.ds(k, 1), :] for k in at]

    for k in (1, 2, 3):
        out, (mine, give) = partial(k, -k)
        start = (k - 1) * FULL
        mine_ref[pl.ds(start, BLOCK), :] = out[:BLOCK]
        mine_ref[pl.ds(start + BLOCK, TAIL), :] = packed(mine)
        give_ref[pl.ds(start, BLOCK), :] = flipped(out[BLOCK:])
        give_ref[pl.ds(start + BLOCK, TAIL), :] = packed(halves_turned(give))
    out, totals = partial(4, 0)
    for side in range(2):
        start = 3 * FULL + side * FAR
        rows = out[side * BLOCK : side * BLOCK + BLOCK]
        mine_ref[pl.ds(start, PIECE), :] = rows[:PIECE]
        mine_ref[pl.ds(start + PIECE, TAIL), :] = packed(totals[side])
        give_ref[pl.ds(start, PIECE), :] = rows[PIECE:]
        give_ref[pl.ds(start + PIECE, TAIL), :] = packed(halves_turned(totals[side]))


def summed(a, b, rows):
    body = a[:rows].astype(jnp.float32) + b[:rows].astype(jnp.float32)
    tail = packed(unpacked(a[rows:]) + unpacked(b[rows:]))
    return jnp.concatenate([body.astype(jnp.bfloat16), tail], axis=0)


def cores_kernel(mine_ref, got_ref, b1_ref, b2_ref, b3_ref, far_ref, home_ref):
    for k, out in enumerate((b1_ref, b2_ref, b3_ref)):
        part = pl.ds(k * FULL, FULL)
        out[...] = summed(mine_ref[part, :], got_ref[part, :], BLOCK)
    for k, out in enumerate((far_ref, home_ref)):
        part = pl.ds(3 * FULL + k * FAR, FAR)
        out[...] = summed(mine_ref[part, :], got_ref[part, :], PIECE)


def far_kernel(block_ref, far_ref, out_ref):
    block, far = block_ref[...], far_ref[...]
    out_ref[pl.ds(0, PIECE), :] = (
        block[:PIECE].astype(jnp.float32) + far[:PIECE].astype(jnp.float32)
    ).astype(jnp.bfloat16)
    out_ref[pl.ds(PIECE, PIECE), :] = block[PIECE:BLOCK]
    first = lax.broadcasted_iota(jnp.int32, (1, 128), 1) < PIECE
    more = jnp.where(first, unpacked(far[PIECE:]), 0.0)
    out_ref[pl.ds(BLOCK, TAIL), :] = packed(unpacked(block[BLOCK:]) + more)


def block_kernel(block_ref, more_ref, out_ref):
    out_ref[...] = summed(block_ref[...], more_ref[...], BLOCK)


def velocity_kernel(last_ref, home_ref, other_ref, noise_ref, out_ref):
    last, home, other = last_ref[...], home_ref[...], other_ref[...]
    body = last[:PIECE].astype(jnp.float32) + home[:PIECE].astype(jnp.float32)
    body = body + other[:PIECE].astype(jnp.float32)
    total = unpacked(last[BLOCK:]) + unpacked(home[PIECE:]) + halves_turned(unpacked(other[PIECE:]))
    target = body / down(total)[:PIECE]
    out_ref[...] = (target - noise_ref[...].astype(jnp.float32)).astype(jnp.bfloat16)


SQUARE = jax.ShapeDtypeStruct((8, 128), jnp.float32)
COPIES = jax.ShapeDtypeStruct((16, 8, 128), jnp.float32)


def in_vmem(rows, dtype):
    return pltpu.VMEM((rows, 1024), dtype)


def run(kernel, outs, *args, flops=0, scratch=()):
    return pl.pallas_call(
        kernel,
        out_shape=outs,
        in_specs=[pl.BlockSpec(memory_space=pltpu.VMEM)] * len(args),
        out_specs=jax.tree.map(lambda _: pl.BlockSpec(memory_space=pltpu.VMEM), outs),
        scratch_shapes=scratch,
        compiler_params=pltpu.CompilerParams(vmem_limit_bytes=40 * 1024 * 1024),
        cost_estimate=pl.CostEstimate(flops=flops, bytes_accessed=4 << 20, transcendentals=0),
    )(*args)


def keep(a):
    return pltpu.with_memory_space_constraint(a, pltpu.VMEM)


def rows_of(count):
    return jax.ShapeDtypeStruct((count, WIDTH), jnp.bfloat16)


def per_device(noise_latents, data_latents):
    columns = gather_columns(data_latents)
    rows = gather_rows(noise_latents)

    scores, parts = run(
        scores_kernel,
        (in_vmem(ROWS, jnp.float32), COPIES),
        *columns,
        *rows,
        scratch=[pltpu.VMEM((8, 128), jnp.float32)],
    )
    scores = keep(scores)
    row_dual, parts = run(columns_kernel, (SQUARE, COPIES), scores, spread(parts, ROW_GROUP))
    plan, parts = run(
        plan_kernel,
        (in_vmem(ROWS, jnp.bfloat16), COPIES),
        scores,
        row_dual,
        spread(parts, COL_GROUP),
    )
    plan = keep(plan)
    parts = run(column_sums_kernel, COPIES, plan, spread(parts, ROW_GROUP))
    parts = run(row_sums_kernel, COPIES, plan, spread(parts, COL_GROUP))
    parts = run(column_sums_kernel, COPIES, plan, spread(parts, ROW_GROUP))
    count = 3 * FULL + 2 * FAR
    mine, give = run(
        targets_kernel,
        (rows_of(count), rows_of(count)),
        plan,
        spread(parts, COL_GROUP),
        *columns,
        scratch=[pltpu.VMEM((ROWS, ROWS), jnp.bfloat16), pltpu.VMEM((8, 128), jnp.float32)],
    )
    b1, b2, b3, far, home = run(
        cores_kernel,
        (rows_of(FULL), rows_of(FULL), rows_of(FULL), rows_of(FAR), rows_of(FAR)),
        mine,
        swap_core(give),
    )
    moving = run(far_kernel, rows_of(FULL), b3, shift_z(far))
    moving = run(block_kernel, rows_of(FULL), b2, shift_z(moving))
    moving = run(block_kernel, rows_of(FULL), b1, shift_z(moving))
    last = shift_z(moving)
    other = swap_core(last[PIECE:])
    return run(velocity_kernel, rows_of(PIECE), last, home, other, noise_latents)


def solution(mesh):
    fine = Mesh(mesh.devices.reshape(SIZES), AXES)
    rows = P(AXES, None)
    return jax.shard_map(
        per_device, mesh=fine, in_specs=(rows, rows), out_specs=rows, check_vma=False
    )
```

```python
import functools
import math

import jax
import jax.numpy as jnp
from jax import lax
from jax.experimental import pallas as pl
from jax.experimental.pallas import tpu as pltpu
from jax.sharding import Mesh
from jax.sharding import PartitionSpec as P

WIDTH = 1024
ROWS = 1024
eps_factor = 0.3

AXES = ("x", "yh", "core", "yl", "z")
SIZES = (4, 2, 2, 2, 8)
ROW_GROUP = ("core", "z")
COL_GROUP = ("x", "yh", "yl")

EPSILON = eps_factor * math.sqrt(WIDTH)
LOG2E = math.log2(math.e)
LOG2_MASS = -math.log2(16384)


PIECE = 64
BLOCK = 2 * PIECE
TAIL = 16
UNIT = PIECE + TAIL


def number(place):
    index = 0
    for size, at in zip(SIZES, place):
        index = index * size + at % size
    return index


def moved(a, move):
    pairs = []
    for x in range(4):
        for y in range(4):
            for core in range(2):
                for z in range(8):
                    tx, ty, tcore, tz = move(x, y, core, z)
                    source = (x, y // 2, core, y % 2, z)
                    pairs.append((number(source), number((tx, ty // 2, tcore, ty % 2, tz))))
    return lax.ppermute(a, AXES, pairs)


def swap_core(a):
    return moved(a, lambda x, y, core, z: (x, y, 1 - core, z))


def shift_z(a):
    return moved(a, lambda x, y, core, z: (x, y, core, z + 1 - 2 * core))


def swap_x(a, flips):
    return moved(a, lambda x, y, core, z: (x ^ flips[core], y, core, z))


def swap_y(a, flips):
    return moved(a, lambda x, y, core, z: (x, y ^ flips[core], core, z))


def spread(copies, group):
    return lax.all_to_all(copies, group, 0, 0)


def side(position):
    core = lax.axis_index("core")
    low, high = position
    return jnp.where(core == 0, low, high), jnp.where(core == 0, high, low ^ high)


def sides():
    x = lax.axis_index("x")
    along_x = side((x % 2, x // 2))
    along_y = side((lax.axis_index("yl"), lax.axis_index("yh")))
    return along_x + along_y, along_y + along_x


def doubled(part, other, at):
    return jnp.where(
        at == 0,
        jnp.concatenate([part, other], axis=0),
        jnp.concatenate([other, part], axis=0),
    )


def gather(noise, data):
    first, second = (1, 3), (3, 1)
    moves = [(swap_x, first), (swap_x, second), (swap_y, first), (swap_y, second)]
    moves = moves, moves[2:] + moves[:2]
    parts = [data[: PIECE // 2], data[PIECE // 2 :]]
    straight, beside = [noise], []
    for step in range(3):
        received = [swap(part, flips) for part, (swap, flips) in zip(parts, [m[step] for m in moves])]
        near = shift_z(straight[-1])
        by = swap_core(noise) if step == 0 else shift_z(beside[-1])
        *received, near, by = lax.optimization_barrier((*received, near, by))
        straight.append(near)
        beside.append(by)
        parts = [
            doubled(part, other, at[step]) for part, other, at in zip(parts, received, sides())
        ]
    pieces = []
    for part, m in zip(parts, moves):
        swap, flips = m[3]
        pieces.append([part, swap(part[:BLOCK], flips), swap(part[BLOCK:], flips)])
    beside.append(shift_z(beside[-1]))
    straight.append(shift_z(straight[-1]))
    early = swap_core(jnp.concatenate([straight[1], beside[1], straight[2], beside[2], straight[3]], axis=0))
    late = swap_core(jnp.concatenate([beside[3], straight[4]], axis=0))
    rows = [noise, beside[0], straight[1], beside[1], straight[2], beside[2]]
    return pieces[0] + pieces[1], rows + [straight[3], beside[3], straight[4], early, late]


def to_lanes(square):
    return jnp.concatenate([square[k : k + 1, :] for k in range(8)], axis=1)


def to_square(lanes):
    return jnp.concatenate([lanes[:, 128 * k : 128 * k + 128] for k in range(8)], axis=0)


def own_first(square):
    swapped = jnp.concatenate([square[:, PIECE:], square[:, :PIECE]], axis=1)
    return jnp.where(lax.axis_index("core") == 0, square, swapped)


def lse2(parts):
    top = jnp.max(parts, axis=0)
    return top + jnp.log2(jnp.sum(jnp.exp2(parts - top[None]), axis=0))


def send(out_ref, square):
    out_ref[...] = jnp.broadcast_to(square[None], (16, 8, 128))


def terms(lanes):
    high = lanes.astype(jnp.bfloat16)
    rest = lanes - high.astype(jnp.float32)
    low = rest.astype(jnp.bfloat16)
    zeros = jnp.zeros((14, ROWS), jnp.bfloat16)
    return jnp.concatenate([high, low, zeros], axis=0)


def down(row):
    return jnp.transpose(jnp.broadcast_to(row, (128, 128)))[:, :1]


def across(column):
    return jnp.transpose(jnp.broadcast_to(column, (128, 128)))[:1, :]


def square_sums(block):
    wide = block.astype(jnp.float32)
    return jnp.sum(wide * wide, axis=1, keepdims=True)


def along_z(steps):
    return jnp.bitwise_and(lax.axis_index("z") + (1 - 2 * lax.axis_index("core")) * steps, 7)


def flipped(block):
    return jnp.concatenate([block[PIECE:], block[:PIECE]], axis=0)


def places():
    starts = []
    for h, at in enumerate(sides()):
        own = 512 * h + 256 * at[3]
        other = 512 * h + 256 - 256 * at[3]
        starts += [own, other, other + BLOCK]
    return [pl.multiple_of(start, BLOCK) for start in starts]


def scores_kernel(d0, d1, d2, d3, d4, d5, n0, b0, n1, b1, n2, b2, n3, b3, n4, early, late, *outs):
    score_ref, out_ref, lse_ref = outs
    scale = LOG2E / EPSILON
    swapped = [early[pl.ds(PIECE * k, PIECE), :] for k in range(5)]
    swapped += [late[pl.ds(PIECE * k, PIECE), :] for k in range(2)]
    pairs = [
        (0, 4, [n0[...], b0[...], n4[...], swapped[6]]),
        (-1, 1, [n1[...], b1[...], swapped[1], swapped[0]]),
        (-2, 2, [n2[...], b2[...], swapped[3], swapped[2]]),
        (-3, 3, [n3[...], b3[...], swapped[5], swapped[4]]),
    ]
    pieces = list(zip((d0, d1, d2, d3, d4, d5), places()))
    data_norms = [
        jnp.concatenate(
            [square_sums(data[pl.ds(at, 128), :]) for at in range(0, data.shape[0], 128)], axis=0
        )
        for data, _ in pieces
    ]
    for first, second, shards in pairs:
        noise = jnp.concatenate(shards, axis=0)
        noise_norms = jnp.concatenate(
            [across(square_sums(noise[:BLOCK])), across(square_sums(noise[BLOCK:]))], axis=1
        )
        found = []
        for (data, _), norms in zip(pieces, data_norms):
            products = lax.dot_general(
                data[...], noise, (((1,), (1,)), ((), ())), preferred_element_type=jnp.float32
            )
            found.append((2.0 * products - (norms + noise_norms)) * scale)
        top = functools.reduce(
            jnp.maximum, [jnp.max(scores, axis=0, keepdims=True) for scores in found]
        )
        total = sum(jnp.sum(jnp.exp2(scores - top), axis=0, keepdims=True) for scores in found)
        row = top + jnp.log2(total)
        for half, steps in enumerate((first, second)):
            at = along_z(steps)
            lanes = slice(BLOCK * half, BLOCK * half + BLOCK)
            lse_ref[pl.ds(at, 1), :] = row[:, lanes]
            columns = pl.ds(pl.multiple_of(at * 128, 128), 128)
            for scores, (data, start) in zip(found, pieces):
                score_ref[pl.ds(start, data.shape[0]), columns] = scores[:, lanes]
    send(out_ref, own_first(lse_ref[...]))


def columns_kernel(score_ref, in_ref, dual_ref, out_ref):
    dual = own_first(LOG2_MASS - lse2(in_ref[...]))
    dual_ref[...] = dual
    along = to_lanes(dual)
    rows = []
    for k in range(8):
        shifted = score_ref[pl.ds(128 * k, 128), :] + along
        top = jnp.max(shifted, axis=1, keepdims=True)
        total = jnp.sum(jnp.exp2(shifted - top), axis=1, keepdims=True)
        rows.append(across(top + jnp.log2(total)))
    send(out_ref, jnp.concatenate(rows, axis=0))


def plan_kernel(score_ref, dual_ref, in_ref, plan_ref, out_ref):
    along = to_lanes(dual_ref[...])
    dual = LOG2_MASS - lse2(in_ref[...])
    sums = jnp.zeros((1, ROWS), jnp.float32)
    for k in range(8):
        part = pl.ds(128 * k, 128)
        lifted = down(dual[k : k + 1, :] - LOG2_MASS)
        plan = jnp.exp2(score_ref[part, :] + along + lifted)
        plan_ref[part, :] = plan.astype(jnp.bfloat16)
        sums = sums + jnp.sum(plan, axis=0, keepdims=True)
    send(out_ref, own_first(to_square(sums)))


def column_sums_kernel(plan_ref, in_ref, out_ref):
    scale = own_first(1.0 / jnp.sum(in_ref[...], axis=0))
    sums = lax.dot_general(
        terms(to_lanes(scale)),
        plan_ref[...],
        (((1,), (1,)), ((), ())),
        preferred_element_type=jnp.float32,
    )
    send(out_ref, to_square(sums[0:1, :] + sums[1:2, :]))


def row_sums_kernel(plan_ref, in_ref, out_ref):
    scale = 1.0 / jnp.sum(in_ref[...], axis=0)
    sums = jnp.dot(terms(to_lanes(scale)), plan_ref[...], preferred_element_type=jnp.float32)
    send(out_ref, own_first(to_square(sums[0:1, :] + sums[1:2, :])))


def packed(total):
    high = total.astype(jnp.bfloat16)
    low = (total - high.astype(jnp.float32)).astype(jnp.bfloat16)
    zeros = jnp.zeros((TAIL - 2, 128), jnp.bfloat16)
    narrow = jnp.concatenate([high, low, zeros], axis=0)
    return jnp.concatenate([narrow, jnp.zeros((TAIL, WIDTH - 128), jnp.bfloat16)], axis=1)


def unpacked(tail):
    return tail[0:1, :128].astype(jnp.float32) + tail[1:2, :128].astype(jnp.float32)


def halves_turned(total):
    return jnp.concatenate([total[:, PIECE:], total[:, :PIECE]], axis=1)


def give_unit(ref, index, rows, total):
    ref[pl.ds(index * UNIT, PIECE), :] = rows
    ref[pl.ds(index * UNIT + PIECE, TAIL), :] = packed(total)


def share(mine, give, index, rows, total):
    give_unit(mine, index, rows[:PIECE], total)
    give_unit(give, index, rows[PIECE:], halves_turned(total))


def whole(ref, index, rows, total, turned):
    parts = [(rows[:PIECE], total), (rows[PIECE:], halves_turned(total))]
    for k, (part, sums) in enumerate(parts[::-1] if turned else parts):
        give_unit(ref, index + k, part, sums)


def pair_targets(weight_ref, sum_ref, pieces, first, second):
    at = [along_z(first), along_z(second)]
    lanes = [pl.ds(pl.multiple_of(k * 128, 128), 128) for k in at]
    out = 0.0
    for data, start in pieces:
        rows = pl.ds(start, data.shape[0])
        weights = jnp.concatenate([weight_ref[rows, part] for part in lanes], axis=1)
        out = out + lax.dot_general(
            weights, data[...], (((0,), (0,)), ((), ())), preferred_element_type=jnp.float32
        )
    out = out.astype(jnp.bfloat16)
    return (out[:BLOCK], sum_ref[pl.ds(at[0], 1), :]), (out[BLOCK:], sum_ref[pl.ds(at[1], 1), :])


def early_targets_kernel(plan_ref, in_ref, d0, d1, d2, d3, d4, d5, *outs):
    weight_ref, sum_ref, mine, give = outs
    scale = 1.0 / jnp.sum(in_ref[...], axis=0)
    sums = jnp.zeros((1, ROWS), jnp.float32)
    for k in range(8):
        part = pl.ds(128 * k, 128)
        weights = plan_ref[part, :].astype(jnp.float32) * down(scale[k : k + 1, :])
        weight_ref[part, :] = weights.astype(jnp.bfloat16)
        sums = sums + jnp.sum(weights, axis=0, keepdims=True)
    sum_ref[...] = to_square(sums)
    pieces = list(zip((d0, d1, d2, d3, d4, d5), places()))
    far, third = pair_targets(weight_ref, sum_ref, pieces, 4, -3)
    share(mine, give, 0, *far)
    whole(give, 1, *third, True)


def late_targets_kernel(weight_ref, sum_ref, d0, d1, d2, d3, d4, d5, mine, give):
    pieces = list(zip((d0, d1, d2, d3, d4, d5), places()))
    two, one = pair_targets(weight_ref, sum_ref, pieces, -2, -1)
    whole(give, 0, *two, True)
    whole(give, 2, *one, True)
    home, third = pair_targets(weight_ref, sum_ref, pieces, 0, 3)
    give_unit(mine, 6, home[0][:PIECE], home[1])
    give_unit(give, 4, home[0][PIECE:], halves_turned(home[1]))
    whole(mine, 0, *third, False)
    two, one = pair_targets(weight_ref, sum_ref, pieces, 2, 1)
    whole(mine, 2, *two, False)
    whole(mine, 4, *one, False)


def summed(a, b):
    body = a[:PIECE].astype(jnp.float32) + b[:PIECE].astype(jnp.float32)
    tail = packed(unpacked(a[PIECE:]) + unpacked(b[PIECE:]))
    return jnp.concatenate([body.astype(jnp.bfloat16), tail], axis=0)


def unit(ref, index):
    return ref[pl.ds(index * UNIT, UNIT), :]


def start_kernel(far, late, got, far_ref, third0_ref, third1_ref):
    far_ref[...] = summed(far[...], unit(got, 0))
    third0_ref[...] = summed(unit(late, 0), unit(got, 1))
    third1_ref[...] = summed(unit(late, 1), unit(got, 2))


def rest_kernel(late, got, *outs):
    for k, out in enumerate(outs):
        out[...] = summed(unit(late, 2 + k), unit(got, k))


def unit_kernel(a_ref, b_ref, out_ref):
    out_ref[...] = summed(a_ref[...], b_ref[...])


def velocity_kernel(last_ref, home_ref, other_ref, noise_ref, out_ref):
    last, home, other = last_ref[...], home_ref[...], other_ref[...]
    body = last[:PIECE].astype(jnp.float32) + home[:PIECE].astype(jnp.float32)
    body = body + other[:PIECE].astype(jnp.float32)
    total = unpacked(last[PIECE:]) + unpacked(home[PIECE:]) + unpacked(other[PIECE:])
    target = body / down(total)[:PIECE]
    out_ref[...] = (target - noise_ref[...].astype(jnp.float32)).astype(jnp.bfloat16)


SQUARE = jax.ShapeDtypeStruct((8, 128), jnp.float32)
COPIES = jax.ShapeDtypeStruct((16, 8, 128), jnp.float32)


def in_vmem(rows, dtype):
    return pltpu.VMEM((rows, 1024), dtype)


def run(kernel, outs, *args, flops=0, scratch=()):
    return pl.pallas_call(
        kernel,
        out_shape=outs,
        in_specs=[pl.BlockSpec(memory_space=pltpu.VMEM)] * len(args),
        out_specs=jax.tree.map(lambda _: pl.BlockSpec(memory_space=pltpu.VMEM), outs),
        scratch_shapes=scratch,
        compiler_params=pltpu.CompilerParams(vmem_limit_bytes=40 * 1024 * 1024),
        cost_estimate=pl.CostEstimate(flops=flops, bytes_accessed=4 << 20, transcendentals=0),
    )(*args)


def keep(a):
    return pltpu.with_memory_space_constraint(a, pltpu.VMEM)


def units(count):
    return jax.ShapeDtypeStruct((count * UNIT, WIDTH), jnp.bfloat16)


def per_device(noise_latents, data_latents):
    columns, rows = gather(noise_latents, data_latents)

    scores, parts = run(
        scores_kernel,
        (in_vmem(ROWS, jnp.float32), COPIES),
        *columns,
        *rows,
        scratch=[pltpu.VMEM((8, 128), jnp.float32)],
    )
    scores = keep(scores)
    row_dual, parts = run(columns_kernel, (SQUARE, COPIES), scores, spread(parts, ROW_GROUP))
    plan, parts = run(
        plan_kernel,
        (in_vmem(ROWS, jnp.bfloat16), COPIES),
        scores,
        row_dual,
        spread(parts, COL_GROUP),
    )
    plan = keep(plan)
    parts = run(column_sums_kernel, COPIES, plan, spread(parts, ROW_GROUP))
    parts = run(row_sums_kernel, COPIES, plan, spread(parts, COL_GROUP))
    parts = run(column_sums_kernel, COPIES, plan, spread(parts, ROW_GROUP))

    weights, sums, far, give = run(
        early_targets_kernel,
        (in_vmem(ROWS, jnp.bfloat16), SQUARE, units(1), units(3)),
        plan,
        spread(parts, COL_GROUP),
        *columns,
    )
    got = swap_core(give)
    late, give = run(late_targets_kernel, (units(7), units(5)), keep(weights), sums, *columns)
    got_late = swap_core(give)
    far, third0, third1 = run(start_kernel, (units(1),) * 3, far, late, got)
    straight, beside = shift_z(far), shift_z(third1)
    two0, two1, one0, one1, home = run(rest_kernel, (units(1),) * 5, late, got_late)

    straight = shift_z(run(unit_kernel, units(1), third0, straight))
    beside = shift_z(run(unit_kernel, units(1), two1, beside))
    straight = shift_z(run(unit_kernel, units(1), two0, straight))
    beside = shift_z(run(unit_kernel, units(1), one1, beside))
    straight = shift_z(run(unit_kernel, units(1), one0, straight))
    other = swap_core(beside)
    velocity = jax.ShapeDtypeStruct((PIECE, WIDTH), jnp.bfloat16)
    return run(velocity_kernel, velocity, straight, home, other, noise_latents)


def solution(mesh):
    fine = Mesh(mesh.devices.reshape(SIZES), AXES)
    rows = P(AXES, None)
    return jax.shard_map(
        per_device, mesh=fine, in_specs=(rows, rows), out_specs=rows, check_vma=False
    )
```

```python
import functools
import math

import jax
import jax.numpy as jnp
from jax import lax
from jax.experimental import pallas as pl
from jax.experimental.pallas import tpu as pltpu
from jax.sharding import Mesh
from jax.sharding import PartitionSpec as P

WIDTH = 1024
ROWS = 1024
PIECE = 64
SENT = WIDTH + 128
eps_factor = 0.3

AXES = ("x", "yh", "core", "yl", "z")
SIZES = (4, 2, 2, 2, 8)
ROW_GROUP = ("core", "z")
COL_GROUP = ("x", "yh", "yl")

EPSILON = eps_factor * math.sqrt(WIDTH)
LOG2E = math.log2(math.e)
LOG2_MASS = -math.log2(16384)


def device_pairs(move):
    pairs = []
    for x in range(4):
        for yh in range(2):
            for core in range(2):
                for yl in range(2):
                    for z in range(8):
                        place = (x, yh, core, yl, z)
                        pairs.append((number(place), number(move(*place))))
    return pairs


def number(place):
    index = 0
    for size, at in zip(SIZES, place):
        index = index * size + at % size
    return index


def shift_z(a, by):
    return lax.ppermute(a, AXES, device_pairs(lambda x, yh, c, yl, z: (x, yh, c, yl, z + by)))


def swap_core(a):
    return lax.ppermute(a, AXES, device_pairs(lambda x, yh, c, yl, z: (x, yh, 1 - c, yl, z)))


def spread(copies, group):
    return lax.all_to_all(copies, group, 0, 0)


def put(whole, part, at):
    return lax.dynamic_update_index_in_dim(whole, part, at, 0)


def gather_z(part):
    z = lax.axis_index("z")
    whole = put(jnp.zeros((8,) + part.shape, part.dtype), part, z)
    right = left = part
    for k in (1, 2, 3, 4):
        right = shift_z(right, 1)
        whole = put(whole, right, jnp.bitwise_and(z - k, 7))
        if k < 4:
            left = shift_z(left, -1)
            whole = put(whole, left, jnp.bitwise_and(z + k, 7))
    return whole


def to_lanes(square):
    return jnp.concatenate([square[k : k + 1, :] for k in range(8)], axis=1)


def to_square(lanes):
    return jnp.concatenate([lanes[:, 128 * k : 128 * k + 128] for k in range(8)], axis=0)


def own_first(square):
    swapped = jnp.concatenate([square[4:, :], square[:4, :]], axis=0)
    return jnp.where(lax.axis_index("core") == 0, square, swapped)


def lse2(parts):
    top = jnp.max(parts, axis=0)
    return top + jnp.log2(jnp.sum(jnp.exp2(parts - top[None]), axis=0))


def send(out_ref, square):
    out_ref[...] = jnp.broadcast_to(square[None], (16, 8, 128))


def terms(lanes):
    high = lanes.astype(jnp.bfloat16)
    rest = lanes - high.astype(jnp.float32)
    low = rest.astype(jnp.bfloat16)
    zeros = jnp.zeros((14, ROWS), jnp.bfloat16)
    return jnp.concatenate([high, low, zeros], axis=0)


def down(row):
    return jnp.transpose(jnp.broadcast_to(row, (128, 128)))[:, :1]


def across(column):
    return jnp.transpose(jnp.broadcast_to(column, (128, 128)))[:1, :]


def square_sums(block):
    wide = block.astype(jnp.float32)
    return jnp.sum(wide * wide, axis=1, keepdims=True)


def scores_kernel(data_ref, own_ref, other_ref, score_ref, out_ref):
    scale = LOG2E / EPSILON
    data_norms = jnp.concatenate(
        [square_sums(data_ref[pl.ds(128 * k, 128), :]) for k in range(8)], axis=0
    )
    rows = []
    for k in range(4):
        source = own_ref if k < 2 else other_ref
        noise = source[pl.ds(256 * (k % 2), 256), :]
        noise_norms = jnp.concatenate(
            [across(square_sums(noise[:128])), across(square_sums(noise[128:]))], axis=1
        )
        products = lax.dot_general(
            data_ref[...], noise, (((1,), (1,)), ((), ())), preferred_element_type=jnp.float32
        )
        scores = (2.0 * products - (data_norms + noise_norms)) * scale
        score_ref[:, pl.ds(256 * k, 256)] = scores
        top = jnp.max(scores, axis=0, keepdims=True)
        total = jnp.sum(jnp.exp2(scores - top), axis=0, keepdims=True)
        rows.append(top + jnp.log2(total))
    send(out_ref, own_first(to_square(jnp.concatenate(rows, axis=1))))


def columns_kernel(score_ref, in_ref, dual_ref, out_ref):
    dual = own_first(LOG2_MASS - lse2(in_ref[...]))
    dual_ref[...] = dual
    along = to_lanes(dual)
    rows = []
    for k in range(8):
        shifted = score_ref[pl.ds(128 * k, 128), :] + along
        top = jnp.max(shifted, axis=1, keepdims=True)
        total = jnp.sum(jnp.exp2(shifted - top), axis=1, keepdims=True)
        rows.append(across(top + jnp.log2(total)))
    send(out_ref, jnp.concatenate(rows, axis=0))


def plan_kernel(score_ref, dual_ref, in_ref, plan_ref, out_ref):
    along = to_lanes(dual_ref[...])
    dual = LOG2_MASS - lse2(in_ref[...])
    sums = jnp.zeros((1, ROWS), jnp.float32)
    for k in range(8):
        part = pl.ds(128 * k, 128)
        lifted = down(dual[k : k + 1, :] - LOG2_MASS)
        plan = jnp.exp2(score_ref[part, :] + along + lifted)
        plan_ref[part, :] = plan.astype(jnp.bfloat16)
        sums = sums + jnp.sum(plan, axis=0, keepdims=True)
    send(out_ref, own_first(to_square(sums)))


def column_sums_kernel(plan_ref, in_ref, out_ref):
    scale = own_first(1.0 / jnp.sum(in_ref[...], axis=0))
    sums = lax.dot_general(
        terms(to_lanes(scale)),
        plan_ref[...],
        (((1,), (1,)), ((), ())),
        preferred_element_type=jnp.float32,
    )
    send(out_ref, to_square(sums[0:1, :] + sums[1:2, :]))


def row_sums_kernel(plan_ref, in_ref, out_ref):
    scale = 1.0 / jnp.sum(in_ref[...], axis=0)
    sums = jnp.dot(terms(to_lanes(scale)), plan_ref[...], preferred_element_type=jnp.float32)
    send(out_ref, own_first(to_square(sums[0:1, :] + sums[1:2, :])))


def copies_kernel(data_ref, out_ref):
    for k in range(16):
        out_ref[k] = data_ref[...]


def with_total(body, total):
    high = total.astype(jnp.bfloat16).astype(jnp.float32)
    first = lax.broadcasted_iota(jnp.int32, total.shape, 1) < 64
    tail = jnp.where(first, high, total - high)
    return jnp.concatenate([body.astype(jnp.bfloat16), tail.astype(jnp.bfloat16)], axis=1)


def body_total(sent):
    tail = sent[:, WIDTH:].astype(jnp.float32)
    return sent[:, :WIDTH].astype(jnp.float32), tail + pltpu.roll(tail, 64, 1)


def summed(a, b):
    (body_a, total_a), (body_b, total_b) = body_total(a), body_total(b)
    return with_total(body_a + body_b, total_a + total_b)


def half_targets(weight_ref, data_ref, start, out_ref):
    ones = jnp.ones((ROWS, 128), jnp.bfloat16)
    for k in range(2):
        weights = weight_ref[:, pl.ds(start + 256 * k, 256)]
        found = [
            lax.dot_general(weights, side, (((0,), (0,)), ((), ())), preferred_element_type=jnp.float32)
            for side in (data_ref[...], ones)
        ]
        out_ref[pl.ds(256 * k, 256), :] = with_total(*found)


def other_targets_kernel(plan_ref, in_ref, data_ref, weight_ref, out_ref):
    scale = 1.0 / jnp.sum(in_ref[...], axis=0)
    for k in range(8):
        part = pl.ds(128 * k, 128)
        weights = plan_ref[part, :].astype(jnp.float32) * down(scale[k : k + 1, :])
        weight_ref[part, :] = weights.astype(jnp.bfloat16)
    half_targets(weight_ref, data_ref, ROWS // 2, out_ref)


def own_targets_kernel(weight_ref, data_ref, out_ref):
    half_targets(weight_ref, data_ref, 0, out_ref)


def piece(ref, offset):
    at = jnp.bitwise_and(lax.axis_index("z") + offset, 7)
    return ref[pl.ds(pl.multiple_of(at * PIECE, PIECE), PIECE), :]


def cores_kernel(own_ref, got_ref, out_ref, right_ref, left_ref):
    for k in range(4):
        part = pl.ds(128 * k, 128)
        out_ref[part, :] = summed(own_ref[part, :], got_ref[part, :])
    right_ref[...] = piece(out_ref, 4)
    left_ref[...] = piece(out_ref, 5)


def pass_kernel(offset, own_ref, got_ref, out_ref):
    out_ref[...] = summed(piece(own_ref, offset), got_ref[...])


def velocity_kernel(own_ref, right_ref, left_ref, noise_ref, out_ref):
    found = [body_total(a) for a in (piece(own_ref, 0), right_ref[...], left_ref[...])]
    body, total = (sum(values) for values in zip(*found))
    target = body / total[:, :1]
    out_ref[...] = (target - noise_ref[...].astype(jnp.float32)).astype(jnp.bfloat16)


SQUARE = jax.ShapeDtypeStruct((8, 128), jnp.float32)
COPIES = jax.ShapeDtypeStruct((16, 8, 128), jnp.float32)


def in_vmem(rows, dtype):
    return pltpu.VMEM((rows, 1024), dtype)


def run(kernel, outs, *args, flops=0, scratch=()):
    return pl.pallas_call(
        kernel,
        out_shape=outs,
        in_specs=[pl.BlockSpec(memory_space=pltpu.VMEM)] * len(args),
        out_specs=jax.tree.map(lambda _: pl.BlockSpec(memory_space=pltpu.VMEM), outs),
        scratch_shapes=scratch,
        compiler_params=pltpu.CompilerParams(vmem_limit_bytes=40 * 1024 * 1024),
        cost_estimate=pl.CostEstimate(flops=flops, bytes_accessed=4 << 20, transcendentals=0),
    )(*args)


def keep(a):
    return pltpu.with_memory_space_constraint(a, pltpu.VMEM)


def sent_rows(count):
    return pltpu.VMEM((count, SENT), jnp.bfloat16)


def per_device(noise_latents, data_latents):
    copies = run(copies_kernel, pltpu.VMEM((16, PIECE, WIDTH), jnp.bfloat16), data_latents)
    copies, noise = lax.optimization_barrier((copies, noise_latents))
    columns = keep(spread(copies, COL_GROUP).reshape(ROWS, WIDTH))
    own_rows = gather_z(noise).reshape(ROWS // 2, WIDTH)
    other_rows = keep(swap_core(own_rows))

    scores, parts = run(
        scores_kernel,
        (in_vmem(ROWS, jnp.float32), COPIES),
        columns,
        keep(own_rows),
        other_rows,
        flops=2 * ROWS * ROWS * WIDTH,
    )
    scores = keep(scores)
    row_dual, parts = run(columns_kernel, (SQUARE, COPIES), scores, spread(parts, ROW_GROUP))
    plan, parts = run(
        plan_kernel,
        (in_vmem(ROWS, jnp.bfloat16), COPIES),
        scores,
        row_dual,
        spread(parts, COL_GROUP),
    )
    plan = keep(plan)
    parts = run(column_sums_kernel, COPIES, plan, spread(parts, ROW_GROUP))
    parts = run(row_sums_kernel, COPIES, plan, spread(parts, COL_GROUP))
    parts = run(column_sums_kernel, COPIES, plan, spread(parts, ROW_GROUP))
    weights, others = run(
        other_targets_kernel,
        (in_vmem(ROWS, jnp.bfloat16), sent_rows(ROWS // 2)),
        plan,
        spread(parts, COL_GROUP),
        columns,
        flops=ROWS * ROWS * WIDTH,
    )
    got = swap_core(others)
    own = run(
        own_targets_kernel,
        sent_rows(ROWS // 2),
        keep(weights),
        columns,
        flops=ROWS * ROWS * WIDTH,
    )
    own, right, left = run(
        cores_kernel,
        (sent_rows(ROWS // 2), sent_rows(PIECE), sent_rows(PIECE)),
        keep(own),
        keep(got),
    )
    own = keep(own)
    right, left = shift_z(right, 1), shift_z(left, -1)
    for k in (3, 2, 1):
        passing = functools.partial(pass_kernel, k)
        right = shift_z(run(passing, sent_rows(PIECE), own, keep(right)), 1)
        if k > 1:
            passing = functools.partial(pass_kernel, 9 - k)
            left = shift_z(run(passing, sent_rows(PIECE), own, keep(left)), -1)
    velocity = jax.ShapeDtypeStruct((PIECE, WIDTH), jnp.bfloat16)
    return run(velocity_kernel, velocity, own, keep(right), keep(left), noise_latents)


def solution(mesh):
    fine = Mesh(mesh.devices.reshape(SIZES), AXES)
    rows = P(AXES, None)
    return jax.shard_map(
        per_device, mesh=fine, in_specs=(rows, rows), out_specs=rows, check_vma=False
    )
```

```python
import functools
import math

import jax
import jax.numpy as jnp
from jax import lax
from jax.experimental import pallas as pl
from jax.experimental.pallas import tpu as pltpu
from jax.sharding import Mesh
from jax.sharding import PartitionSpec as P

WIDTH = 1024
ROWS = 1024
PIECE = 64
SENT = WIDTH + 128
eps_factor = 0.3

AXES = ("x", "yh", "core", "yl", "z")
SIZES = (4, 2, 2, 2, 8)
ROW_GROUP = ("core", "z")
COL_GROUP = ("x", "yh", "yl")

EPSILON = eps_factor * math.sqrt(WIDTH)
LOG2E = math.log2(math.e)
LOG2_MASS = -math.log2(16384)


def device_pairs(move):
    pairs = []
    for x in range(4):
        for yh in range(2):
            for core in range(2):
                for yl in range(2):
                    for z in range(8):
                        place = (x, yh, core, yl, z)
                        pairs.append((number(place), number(move(*place))))
    return pairs


def number(place):
    index = 0
    for size, at in zip(SIZES, place):
        index = index * size + at % size
    return index


def shift_z(a, by):
    return lax.ppermute(a, AXES, device_pairs(lambda x, yh, c, yl, z: (x, yh, c, yl, z + by)))


def swap_core(a):
    return lax.ppermute(a, AXES, device_pairs(lambda x, yh, c, yl, z: (x, yh, 1 - c, yl, z)))


def spread(copies, group):
    return lax.all_to_all(copies, group, 0, 0)


def put(whole, part, at):
    return lax.dynamic_update_index_in_dim(whole, part, at, 0)


def gather_z(part):
    z = lax.axis_index("z")
    whole = put(jnp.zeros((8,) + part.shape, part.dtype), part, z)
    right = left = part
    for k in (1, 2, 3):
        if k == 3:
            halves = shift_z(right[: PIECE // 2], 2), shift_z(left[PIECE // 2 :], -2)
        right, left = shift_z(right, 1), shift_z(left, -1)
        whole = put(whole, right, jnp.bitwise_and(z - k, 7))
        whole = put(whole, left, jnp.bitwise_and(z + k, 7))
    return put(whole, jnp.concatenate(halves, axis=0), jnp.bitwise_and(z + 4, 7))


def to_lanes(square):
    return jnp.concatenate([square[k : k + 1, :] for k in range(8)], axis=1)


def to_square(lanes):
    return jnp.concatenate([lanes[:, 128 * k : 128 * k + 128] for k in range(8)], axis=0)


def own_first(square):
    swapped = jnp.concatenate([square[4:, :], square[:4, :]], axis=0)
    return jnp.where(lax.axis_index("core") == 0, square, swapped)


def lse2(parts):
    top = jnp.max(parts, axis=0)
    return top + jnp.log2(jnp.sum(jnp.exp2(parts - top[None]), axis=0))


def send(out_ref, square):
    out_ref[...] = jnp.broadcast_to(square[None], (16, 8, 128))


def terms(lanes):
    high = lanes.astype(jnp.bfloat16)
    rest = lanes - high.astype(jnp.float32)
    low = rest.astype(jnp.bfloat16)
    zeros = jnp.zeros((14, ROWS), jnp.bfloat16)
    return jnp.concatenate([high, low, zeros], axis=0)


def down(row):
    return jnp.transpose(jnp.broadcast_to(row, (128, 128)))[:, :1]


def across(column):
    return jnp.transpose(jnp.broadcast_to(column, (128, 128)))[:1, :]


def square_sums(block):
    wide = block.astype(jnp.float32)
    return jnp.sum(wide * wide, axis=1, keepdims=True)


def scores_kernel(data_ref, own_ref, far_ref, score_ref, out_ref, other_ref, sem):
    scale = LOG2E / EPSILON
    load = pltpu.make_async_copy(far_ref, other_ref, sem)
    load.start()
    data_norms = jnp.concatenate(
        [square_sums(data_ref[pl.ds(128 * k, 128), :]) for k in range(8)], axis=0
    )
    rows = []
    for k in range(4):
        if k == 2:
            load.wait()
        source = own_ref if k < 2 else other_ref
        noise = source[pl.ds(256 * (k % 2), 256), :]
        noise_norms = jnp.concatenate(
            [across(square_sums(noise[:128])), across(square_sums(noise[128:]))], axis=1
        )
        products = lax.dot_general(
            data_ref[...], noise, (((1,), (1,)), ((), ())), preferred_element_type=jnp.float32
        )
        scores = (2.0 * products - (data_norms + noise_norms)) * scale
        score_ref[:, pl.ds(256 * k, 256)] = scores
        top = jnp.max(scores, axis=0, keepdims=True)
        total = jnp.sum(jnp.exp2(scores - top), axis=0, keepdims=True)
        rows.append(top + jnp.log2(total))
    send(out_ref, own_first(to_square(jnp.concatenate(rows, axis=1))))


def columns_kernel(score_ref, in_ref, dual_ref, out_ref):
    dual = own_first(LOG2_MASS - lse2(in_ref[...]))
    dual_ref[...] = dual
    along = to_lanes(dual)
    rows = []
    for k in range(8):
        shifted = score_ref[pl.ds(128 * k, 128), :] + along
        top = jnp.max(shifted, axis=1, keepdims=True)
        total = jnp.sum(jnp.exp2(shifted - top), axis=1, keepdims=True)
        rows.append(across(top + jnp.log2(total)))
    send(out_ref, jnp.concatenate(rows, axis=0))


def plan_kernel(score_ref, dual_ref, in_ref, plan_ref, out_ref):
    along = to_lanes(dual_ref[...])
    dual = LOG2_MASS - lse2(in_ref[...])
    sums = jnp.zeros((1, ROWS), jnp.float32)
    for k in range(8):
        part = pl.ds(128 * k, 128)
        lifted = down(dual[k : k + 1, :] - LOG2_MASS)
        plan = jnp.exp2(score_ref[part, :] + along + lifted)
        plan_ref[part, :] = plan.astype(jnp.bfloat16)
        sums = sums + jnp.sum(plan, axis=0, keepdims=True)
    send(out_ref, own_first(to_square(sums)))


def column_sums_kernel(plan_ref, in_ref, out_ref):
    scale = own_first(1.0 / jnp.sum(in_ref[...], axis=0))
    sums = lax.dot_general(
        terms(to_lanes(scale)),
        plan_ref[...],
        (((1,), (1,)), ((), ())),
        preferred_element_type=jnp.float32,
    )
    send(out_ref, to_square(sums[0:1, :] + sums[1:2, :]))


def row_sums_kernel(plan_ref, in_ref, out_ref):
    scale = 1.0 / jnp.sum(in_ref[...], axis=0)
    sums = jnp.dot(terms(to_lanes(scale)), plan_ref[...], preferred_element_type=jnp.float32)
    send(out_ref, own_first(to_square(sums[0:1, :] + sums[1:2, :])))


def copies_kernel(data_ref, out_ref, sems):
    writes = [pltpu.make_async_copy(data_ref, out_ref.at[k], sems.at[k]) for k in range(16)]
    for write in writes:
        write.start()
    for write in writes:
        write.wait()


def with_total(body, total):
    high = total.astype(jnp.bfloat16).astype(jnp.float32)
    first = lax.broadcasted_iota(jnp.int32, total.shape, 1) < 64
    tail = jnp.where(first, high, total - high)
    return jnp.concatenate([body.astype(jnp.bfloat16), tail.astype(jnp.bfloat16)], axis=1)


def body_total(sent):
    tail = sent[:, WIDTH:].astype(jnp.float32)
    return sent[:, :WIDTH].astype(jnp.float32), tail + pltpu.roll(tail, 64, 1)


def summed(a, b):
    (body_a, total_a), (body_b, total_b) = body_total(a), body_total(b)
    return with_total(body_a + body_b, total_a + total_b)


def half_targets(weight_ref, data_ref, start, out_ref):
    ones = jnp.ones((ROWS, 128), jnp.bfloat16)
    for k in range(2):
        weights = weight_ref[:, pl.ds(start + 256 * k, 256)]
        found = [
            lax.dot_general(weights, side, (((0,), (0,)), ((), ())), preferred_element_type=jnp.float32)
            for side in (data_ref[...], ones)
        ]
        out_ref[pl.ds(256 * k, 256), :] = with_total(*found)


def other_targets_kernel(plan_ref, in_ref, data_ref, weight_ref, out_ref):
    scale = 1.0 / jnp.sum(in_ref[...], axis=0)
    for k in range(8):
        part = pl.ds(128 * k, 128)
        weights = plan_ref[part, :].astype(jnp.float32) * down(scale[k : k + 1, :])
        weight_ref[part, :] = weights.astype(jnp.bfloat16)
    half_targets(weight_ref, data_ref, ROWS // 2, out_ref)


def own_targets_kernel(weight_ref, data_ref, out_ref):
    half_targets(weight_ref, data_ref, 0, out_ref)


def piece(ref, offset):
    at = jnp.bitwise_and(lax.axis_index("z") + offset, 7)
    return ref[pl.ds(pl.multiple_of(at * PIECE, PIECE), PIECE), :]


def cores_kernel(own_ref, got_ref, out_ref, right_ref, left_ref, right2_ref, left2_ref):
    for k in range(4):
        part = pl.ds(128 * k, 128)
        out_ref[part, :] = summed(own_ref[part, :], got_ref[part, :])
    right_ref[...] = piece(out_ref, 3)
    left_ref[...] = piece(out_ref, 5)
    far = piece(out_ref, 4)
    right2_ref[...] = far[: PIECE // 2]
    left2_ref[...] = far[PIECE // 2 :]


def join_kernel(offset, start, own_ref, got_ref, far_ref, out_ref):
    found = summed(piece(own_ref, offset), got_ref[...])
    halves = [found[: PIECE // 2], found[PIECE // 2 :]]
    halves[start] = summed(halves[start], far_ref[...])
    out_ref[...] = jnp.concatenate(halves, axis=0)


def pass_kernel(offset, own_ref, got_ref, out_ref):
    out_ref[...] = summed(piece(own_ref, offset), got_ref[...])


def velocity_kernel(own_ref, right_ref, left_ref, noise_ref, out_ref):
    found = [body_total(a) for a in (piece(own_ref, 0), right_ref[...], left_ref[...])]
    body, total = (sum(values) for values in zip(*found))
    target = body / total[:, :1]
    out_ref[...] = (target - noise_ref[...].astype(jnp.float32)).astype(jnp.bfloat16)


SQUARE = jax.ShapeDtypeStruct((8, 128), jnp.float32)
COPIES = jax.ShapeDtypeStruct((16, 8, 128), jnp.float32)


def in_vmem(rows, dtype):
    return pltpu.VMEM((rows, 1024), dtype)


def run(kernel, outs, *args, flops=0, scratch=(), out_space=pltpu.VMEM, in_hbm=()):
    spaces = [pltpu.HBM if k in in_hbm else pltpu.VMEM for k in range(len(args))]
    return pl.pallas_call(
        kernel,
        out_shape=outs,
        in_specs=[pl.BlockSpec(memory_space=space) for space in spaces],
        out_specs=jax.tree.map(lambda _: pl.BlockSpec(memory_space=out_space), outs),
        scratch_shapes=scratch,
        compiler_params=pltpu.CompilerParams(vmem_limit_bytes=40 * 1024 * 1024),
        cost_estimate=pl.CostEstimate(flops=flops, bytes_accessed=4 << 20, transcendentals=0),
    )(*args)


def keep(a):
    return pltpu.with_memory_space_constraint(a, pltpu.VMEM)


def sent_rows(count):
    return pltpu.VMEM((count, SENT), jnp.bfloat16)


def per_device(noise_latents, data_latents):
    copies = run(
        copies_kernel,
        pltpu.HBM((16, PIECE, WIDTH), jnp.bfloat16),
        data_latents,
        scratch=[pltpu.SemaphoreType.DMA((16,))],
        out_space=pltpu.HBM,
    )
    copies, noise = lax.optimization_barrier((copies, noise_latents))
    columns = keep(spread(copies, COL_GROUP).reshape(ROWS, WIDTH))
    own_rows = gather_z(noise).reshape(ROWS // 2, WIDTH)
    other_rows = pltpu.with_memory_space_constraint(swap_core(own_rows), pltpu.HBM)

    scores, parts = run(
        scores_kernel,
        (in_vmem(ROWS, jnp.float32), COPIES),
        columns,
        keep(own_rows),
        other_rows,
        flops=2 * ROWS * ROWS * WIDTH,
        scratch=[pltpu.VMEM((ROWS // 2, WIDTH), jnp.bfloat16), pltpu.SemaphoreType.DMA],
        in_hbm=(2,),
    )
    scores = keep(scores)
    row_dual, parts = run(columns_kernel, (SQUARE, COPIES), scores, spread(parts, ROW_GROUP))
    plan, parts = run(
        plan_kernel,
        (in_vmem(ROWS, jnp.bfloat16), COPIES),
        scores,
        row_dual,
        spread(parts, COL_GROUP),
    )
    plan = keep(plan)
    parts = run(column_sums_kernel, COPIES, plan, spread(parts, ROW_GROUP))
    parts = run(row_sums_kernel, COPIES, plan, spread(parts, COL_GROUP))
    parts = run(column_sums_kernel, COPIES, plan, spread(parts, ROW_GROUP))
    weights, others = run(
        other_targets_kernel,
        (in_vmem(ROWS, jnp.bfloat16), sent_rows(ROWS // 2)),
        plan,
        spread(parts, COL_GROUP),
        columns,
        flops=ROWS * ROWS * WIDTH,
    )
    got = swap_core(others)
    own = run(
        own_targets_kernel,
        sent_rows(ROWS // 2),
        keep(weights),
        columns,
        flops=ROWS * ROWS * WIDTH,
    )
    own, right, left, right2, left2 = run(
        cores_kernel,
        tuple(sent_rows(count) for count in (ROWS // 2, PIECE, PIECE, PIECE // 2, PIECE // 2)),
        keep(own),
        keep(got),
    )
    own = keep(own)
    right, left = shift_z(right, 1), shift_z(left, -1)
    right2, left2 = shift_z(right2, 2), shift_z(left2, -2)
    joined = sent_rows(PIECE)
    right = shift_z(run(functools.partial(join_kernel, 2, 0), joined, own, keep(right), keep(right2)), 1)
    left = shift_z(run(functools.partial(join_kernel, 6, 1), joined, own, keep(left), keep(left2)), -1)
    right = shift_z(run(functools.partial(pass_kernel, 1), joined, own, keep(right)), 1)
    left = shift_z(run(functools.partial(pass_kernel, 7), joined, own, keep(left)), -1)
    velocity = jax.ShapeDtypeStruct((PIECE, WIDTH), jnp.bfloat16)
    return run(velocity_kernel, velocity, own, keep(right), keep(left), noise_latents)


def solution(mesh):
    fine = Mesh(mesh.devices.reshape(SIZES), AXES)
    rows = P(AXES, None)
    return jax.shard_map(
        per_device, mesh=fine, in_specs=(rows, rows), out_specs=rows, check_vma=False
    )
```

```python
import functools
import math

import jax
import jax.numpy as jnp
from jax import lax
from jax.experimental import pallas as pl
from jax.experimental.pallas import tpu as pltpu
from jax.sharding import Mesh
from jax.sharding import PartitionSpec as P

WIDTH = 1024
ROWS = 1024
PIECE = 64
SENT = WIDTH + 128
eps_factor = 0.3

AXES = ("x", "yh", "core", "yl", "z")
SIZES = (4, 2, 2, 2, 8)
ROW_GROUP = ("core", "z")
COL_GROUP = ("x", "yh", "yl")

EPSILON = eps_factor * math.sqrt(WIDTH)
LOG2E = math.log2(math.e)
LOG2_MASS = -math.log2(16384)


def device_pairs(move):
    pairs = []
    for x in range(4):
        for yh in range(2):
            for core in range(2):
                for yl in range(2):
                    for z in range(8):
                        place = (x, yh, core, yl, z)
                        pairs.append((number(place), number(move(*place))))
    return pairs


def number(place):
    index = 0
    for size, at in zip(SIZES, place):
        index = index * size + at % size
    return index


def shift_z(a, by):
    return lax.ppermute(a, AXES, device_pairs(lambda x, yh, c, yl, z: (x, yh, c, yl, z + by)))


def swap_core(a):
    return lax.ppermute(a, AXES, device_pairs(lambda x, yh, c, yl, z: (x, yh, 1 - c, yl, z)))


def spread(copies, group):
    return lax.all_to_all(copies, group, 0, 0)


def shift_out(a, by):
    return lax.ppermute(
        a, AXES, device_pairs(lambda x, yh, c, yl, z: (x, yh, c, yl, z + by * (1 - 2 * c)))
    )


def gather_z(shard):
    ahead, behind = [shard], [shard]
    for step in range(3):
        if step == 2:
            far = shift_out(ahead[2], 2)
        ahead.append(shift_out(ahead[-1], 1))
        behind.append(shift_out(behind[-1], -1))
    return ahead[1], behind[1], ahead[2], behind[2], ahead[3], behind[3], far


FOUND = (-1, 1, -2, 2, -3, 3, 4)


def chip_rows(steps):
    at = lax.axis_index("z") + steps * (1 - 2 * lax.axis_index("core"))
    return pl.ds(pl.multiple_of(jnp.bitwise_and(at, 7) * PIECE, PIECE), PIECE)


def to_lanes(square):
    return jnp.concatenate([square[k : k + 1, :] for k in range(8)], axis=1)


def to_square(lanes):
    return jnp.concatenate([lanes[:, 128 * k : 128 * k + 128] for k in range(8)], axis=0)


def own_first(square):
    swapped = jnp.concatenate([square[4:, :], square[:4, :]], axis=0)
    return jnp.where(lax.axis_index("core") == 0, square, swapped)


def lse2(parts):
    top = jnp.max(parts, axis=0)
    return top + jnp.log2(jnp.sum(jnp.exp2(parts - top[None]), axis=0))


def send(out_ref, square):
    out_ref[...] = jnp.broadcast_to(square[None], (16, 8, 128))


def terms(lanes):
    high = lanes.astype(jnp.bfloat16)
    rest = lanes - high.astype(jnp.float32)
    low = rest.astype(jnp.bfloat16)
    zeros = jnp.zeros((14, ROWS), jnp.bfloat16)
    return jnp.concatenate([high, low, zeros], axis=0)


def down(row):
    return jnp.transpose(jnp.broadcast_to(row, (128, 128)))[:, :1]


def across(column):
    return jnp.transpose(jnp.broadcast_to(column, (128, 128)))[:1, :]


def square_sums(block):
    wide = block.astype(jnp.float32)
    return jnp.sum(wide * wide, axis=1, keepdims=True)


def scores_kernel(data_ref, own_ref, far_ref, score_ref, out_ref, other_ref, sem):
    scale = LOG2E / EPSILON
    load = pltpu.make_async_copy(far_ref, other_ref, sem)
    load.start()
    data_norms = jnp.concatenate(
        [square_sums(data_ref[pl.ds(128 * k, 128), :]) for k in range(8)], axis=0
    )
    rows = []
    for k in range(4):
        if k == 2:
            load.wait()
        source = own_ref if k < 2 else other_ref
        noise = source[pl.ds(256 * (k % 2), 256), :]
        noise_norms = jnp.concatenate(
            [across(square_sums(noise[:128])), across(square_sums(noise[128:]))], axis=1
        )
        products = lax.dot_general(
            data_ref[...], noise, (((1,), (1,)), ((), ())), preferred_element_type=jnp.float32
        )
        scores = (2.0 * products - (data_norms + noise_norms)) * scale
        score_ref[:, pl.ds(256 * k, 256)] = scores
        top = jnp.max(scores, axis=0, keepdims=True)
        total = jnp.sum(jnp.exp2(scores - top), axis=0, keepdims=True)
        rows.append(top + jnp.log2(total))
    send(out_ref, own_first(to_square(jnp.concatenate(rows, axis=1))))


def columns_kernel(score_ref, in_ref, dual_ref, out_ref):
    dual = own_first(LOG2_MASS - lse2(in_ref[...]))
    dual_ref[...] = dual
    along = to_lanes(dual)
    rows = []
    for k in range(8):
        shifted = score_ref[pl.ds(128 * k, 128), :] + along
        top = jnp.max(shifted, axis=1, keepdims=True)
        total = jnp.sum(jnp.exp2(shifted - top), axis=1, keepdims=True)
        rows.append(across(top + jnp.log2(total)))
    send(out_ref, jnp.concatenate(rows, axis=0))


def plan_kernel(score_ref, dual_ref, in_ref, plan_ref, out_ref):
    along = to_lanes(dual_ref[...])
    dual = LOG2_MASS - lse2(in_ref[...])
    sums = jnp.zeros((1, ROWS), jnp.float32)
    for k in range(8):
        part = pl.ds(128 * k, 128)
        lifted = down(dual[k : k + 1, :] - LOG2_MASS)
        plan = jnp.exp2(score_ref[part, :] + along + lifted)
        plan_ref[part, :] = plan.astype(jnp.bfloat16)
        sums = sums + jnp.sum(plan, axis=0, keepdims=True)
    send(out_ref, own_first(to_square(sums)))


def column_sums_kernel(plan_ref, in_ref, out_ref):
    scale = own_first(1.0 / jnp.sum(in_ref[...], axis=0))
    sums = lax.dot_general(
        terms(to_lanes(scale)),
        plan_ref[...],
        (((1,), (1,)), ((), ())),
        preferred_element_type=jnp.float32,
    )
    send(out_ref, to_square(sums[0:1, :] + sums[1:2, :]))


def row_sums_kernel(plan_ref, in_ref, out_ref):
    scale = 1.0 / jnp.sum(in_ref[...], axis=0)
    sums = jnp.dot(terms(to_lanes(scale)), plan_ref[...], preferred_element_type=jnp.float32)
    send(out_ref, own_first(to_square(sums[0:1, :] + sums[1:2, :])))


def copies_kernel(data_ref, out_ref, sems):
    writes = [pltpu.make_async_copy(data_ref, out_ref.at[k], sems.at[k]) for k in range(16)]
    for write in writes:
        write.start()
    for write in writes:
        write.wait()


def tile_kernel(shard_ref, *refs):
    sources, (out_ref, sems) = refs[:7], refs[7:]
    loads = [
        pltpu.make_async_copy(source, out_ref.at[chip_rows(steps), :], sems.at[k])
        for k, (source, steps) in enumerate(zip((shard_ref, *sources), (0, *FOUND)))
    ]
    for load in loads:
        load.start()
    for load in loads:
        load.wait()


def with_total(body, total):
    high = total.astype(jnp.bfloat16).astype(jnp.float32)
    first = lax.broadcasted_iota(jnp.int32, total.shape, 1) < 64
    tail = jnp.where(first, high, total - high)
    return jnp.concatenate([body.astype(jnp.bfloat16), tail.astype(jnp.bfloat16)], axis=1)


def body_total(sent):
    tail = sent[:, WIDTH:].astype(jnp.float32)
    return sent[:, :WIDTH].astype(jnp.float32), tail + pltpu.roll(tail, 64, 1)


def summed(a, b):
    (body_a, total_a), (body_b, total_b) = body_total(a), body_total(b)
    return with_total(body_a + body_b, total_a + total_b)


def half_targets(weight_ref, data_ref, start, out_ref):
    ones = jnp.ones((ROWS, 128), jnp.bfloat16)
    for k in range(2):
        weights = weight_ref[:, pl.ds(start + 256 * k, 256)]
        found = [
            lax.dot_general(weights, side, (((0,), (0,)), ((), ())), preferred_element_type=jnp.float32)
            for side in (data_ref[...], ones)
        ]
        out_ref[pl.ds(256 * k, 256), :] = with_total(*found)


def other_targets_kernel(plan_ref, in_ref, data_ref, weight_ref, out_ref):
    scale = 1.0 / jnp.sum(in_ref[...], axis=0)
    for k in range(8):
        part = pl.ds(128 * k, 128)
        weights = plan_ref[part, :].astype(jnp.float32) * down(scale[k : k + 1, :])
        weight_ref[part, :] = weights.astype(jnp.bfloat16)
    half_targets(weight_ref, data_ref, ROWS // 2, out_ref)


def own_targets_kernel(weight_ref, data_ref, out_ref):
    half_targets(weight_ref, data_ref, 0, out_ref)


def piece(ref, offset):
    at = jnp.bitwise_and(lax.axis_index("z") + offset, 7)
    return ref[pl.ds(pl.multiple_of(at * PIECE, PIECE), PIECE), :]


def start_kernel(own_ref, got_ref, right_ref, left_ref, right2_ref, left2_ref):
    right_ref[...] = summed(piece(own_ref, 3), piece(got_ref, 3))
    left_ref[...] = summed(piece(own_ref, 5), piece(got_ref, 5))
    far = summed(piece(own_ref, 4), piece(got_ref, 4))
    right2_ref[...] = far[: PIECE // 2]
    left2_ref[...] = far[PIECE // 2 :]


def cores_kernel(own_ref, got_ref, out_ref):
    for k, steps in enumerate(LATE):
        out_ref[pl.ds(PIECE * k, PIECE), :] = summed(piece(own_ref, steps), piece(got_ref, steps))


LATE = (0, 1, 2, 6, 7)


def later(ref, steps):
    return ref[pl.ds(PIECE * LATE.index(steps), PIECE), :]


def join_kernel(offset, start, own_ref, got_ref, far_ref, out_ref):
    found = summed(later(own_ref, offset), got_ref[...])
    halves = [found[: PIECE // 2], found[PIECE // 2 :]]
    halves[start] = summed(halves[start], far_ref[...])
    out_ref[...] = jnp.concatenate(halves, axis=0)


def pass_kernel(offset, own_ref, got_ref, out_ref):
    out_ref[...] = summed(later(own_ref, offset), got_ref[...])


def velocity_kernel(own_ref, right_ref, left_ref, noise_ref, out_ref):
    found = [body_total(a) for a in (later(own_ref, 0), right_ref[...], left_ref[...])]
    body, total = (sum(values) for values in zip(*found))
    target = body / total[:, :1]
    out_ref[...] = (target - noise_ref[...].astype(jnp.float32)).astype(jnp.bfloat16)


SQUARE = jax.ShapeDtypeStruct((8, 128), jnp.float32)
COPIES = jax.ShapeDtypeStruct((16, 8, 128), jnp.float32)


def in_vmem(rows, dtype):
    return pltpu.VMEM((rows, 1024), dtype)


def run(kernel, outs, *args, flops=0, scratch=(), out_space=pltpu.VMEM, in_hbm=()):
    spaces = [pltpu.HBM if k in in_hbm else pltpu.VMEM for k in range(len(args))]
    return pl.pallas_call(
        kernel,
        out_shape=outs,
        in_specs=[pl.BlockSpec(memory_space=space) for space in spaces],
        out_specs=jax.tree.map(lambda _: pl.BlockSpec(memory_space=out_space), outs),
        scratch_shapes=scratch,
        compiler_params=pltpu.CompilerParams(vmem_limit_bytes=40 * 1024 * 1024),
        cost_estimate=pl.CostEstimate(flops=flops, bytes_accessed=4 << 20, transcendentals=0),
    )(*args)


def keep(a):
    return pltpu.with_memory_space_constraint(a, pltpu.VMEM)


def sent_rows(count):
    return pltpu.VMEM((count, SENT), jnp.bfloat16)


def per_device(noise_latents, data_latents):
    copies = run(
        copies_kernel,
        pltpu.HBM((16, PIECE, WIDTH), jnp.bfloat16),
        data_latents,
        scratch=[pltpu.SemaphoreType.DMA((16,))],
        out_space=pltpu.HBM,
        in_hbm=(0,),
    )
    columns = keep(spread(copies, COL_GROUP).reshape(ROWS, WIDTH))
    found = lax.cond(
        lax.axis_index("x") < 4, gather_z, lambda shard: (jnp.zeros_like(shard),) * 7, noise_latents
    )
    own_rows = run(
        tile_kernel,
        in_vmem(ROWS // 2, jnp.bfloat16),
        noise_latents,
        *found,
        scratch=[pltpu.SemaphoreType.DMA((8,))],
        in_hbm=range(8),
    )
    other_rows = pltpu.with_memory_space_constraint(swap_core(own_rows), pltpu.HBM)

    scores, parts = run(
        scores_kernel,
        (in_vmem(ROWS, jnp.float32), COPIES),
        columns,
        keep(own_rows),
        other_rows,
        flops=2 * ROWS * ROWS * WIDTH,
        scratch=[pltpu.VMEM((ROWS // 2, WIDTH), jnp.bfloat16), pltpu.SemaphoreType.DMA],
        in_hbm=(2,),
    )
    scores = keep(scores)
    row_dual, parts = run(columns_kernel, (SQUARE, COPIES), scores, spread(parts, ROW_GROUP))
    plan, parts = run(
        plan_kernel,
        (in_vmem(ROWS, jnp.bfloat16), COPIES),
        scores,
        row_dual,
        spread(parts, COL_GROUP),
    )
    plan = keep(plan)
    parts = run(column_sums_kernel, COPIES, plan, spread(parts, ROW_GROUP))
    parts = run(row_sums_kernel, COPIES, plan, spread(parts, COL_GROUP))
    parts = run(column_sums_kernel, COPIES, plan, spread(parts, ROW_GROUP))
    weights, others = run(
        other_targets_kernel,
        (in_vmem(ROWS, jnp.bfloat16), sent_rows(ROWS // 2)),
        plan,
        spread(parts, COL_GROUP),
        columns,
        flops=ROWS * ROWS * WIDTH,
    )
    got = swap_core(others)
    own = run(
        own_targets_kernel,
        sent_rows(ROWS // 2),
        keep(weights),
        columns,
        flops=ROWS * ROWS * WIDTH,
    )
    own, got = keep(own), keep(got)
    right, left, right2, left2 = run(
        start_kernel,
        tuple(sent_rows(count) for count in (PIECE, PIECE, PIECE // 2, PIECE // 2)),
        own,
        got,
    )
    own = run(cores_kernel, sent_rows(PIECE * len(LATE)), own, got)
    own = keep(own)
    right, left = shift_z(right, 1), shift_z(left, -1)
    right2, left2 = shift_z(right2, 2), shift_z(left2, -2)
    joined = sent_rows(PIECE)
    right = shift_z(run(functools.partial(join_kernel, 2, 0), joined, own, keep(right), keep(right2)), 1)
    left = shift_z(run(functools.partial(join_kernel, 6, 1), joined, own, keep(left), keep(left2)), -1)
    right = shift_z(run(functools.partial(pass_kernel, 1), joined, own, keep(right)), 1)
    left = shift_z(run(functools.partial(pass_kernel, 7), joined, own, keep(left)), -1)
    velocity = jax.ShapeDtypeStruct((PIECE, WIDTH), jnp.bfloat16)
    return run(velocity_kernel, velocity, own, keep(right), keep(left), noise_latents)


def solution(mesh):
    fine = Mesh(mesh.devices.reshape(SIZES), AXES)
    rows = P(AXES, None)
    return jax.shard_map(
        per_device, mesh=fine, in_specs=(rows, rows), out_specs=rows, check_vma=False
    )
```

```python
import functools
import math

import jax
import jax.numpy as jnp
from jax import lax
from jax.experimental import pallas as pl
from jax.experimental.pallas import tpu as pltpu
from jax.sharding import Mesh
from jax.sharding import PartitionSpec as P

WIDTH = 1024
ROWS = 1024
PIECE = 64
SENT = WIDTH + 128
eps_factor = 0.3

AXES = ("x", "yh", "core", "yl", "z")
SIZES = (4, 2, 2, 2, 8)
ROW_GROUP = ("z", "core")
COL_GROUP = ("x", "yh", "yl")

EPSILON = eps_factor * math.sqrt(WIDTH)
LOG2E = math.log2(math.e)
LOG2_MASS = -math.log2(16384)


def device_pairs(move):
    pairs = []
    for x in range(4):
        for yh in range(2):
            for core in range(2):
                for yl in range(2):
                    for z in range(8):
                        place = (x, yh, core, yl, z)
                        pairs.append((number(place), number(move(*place))))
    return pairs


def number(place):
    index = 0
    for size, at in zip(SIZES, place):
        index = index * size + at % size
    return index


def shift_z(a, by):
    return lax.ppermute(a, AXES, device_pairs(lambda x, yh, c, yl, z: (x, yh, c, yl, z + by)))


def swap_core(a):
    return lax.ppermute(a, AXES, device_pairs(lambda x, yh, c, yl, z: (x, yh, 1 - c, yl, z)))


def spread(copies, group):
    return lax.all_to_all(copies, group, 0, 0)


def shift_out(a, by):
    return lax.ppermute(
        a, AXES, device_pairs(lambda x, yh, c, yl, z: (x, yh, c, yl, z + by * (1 - 2 * c)))
    )


def gather_z(shard):
    ahead, behind = shift_out(shard, 1), shift_out(shard, -1)
    ahead2, behind2 = shift_out(shard, 2), shift_out(shard, -2)
    far = shift_out(ahead2, 2)
    return ahead, behind, ahead2, behind2, shift_out(ahead2, 1), shift_out(behind2, -1), far


FOUND = (-1, 1, -2, 2, -3, 3, 4)


def chip_rows(steps):
    at = lax.axis_index("z") + steps * (1 - 2 * lax.axis_index("core"))
    return pl.ds(pl.multiple_of(jnp.bitwise_and(at, 7) * PIECE, PIECE), PIECE)


def to_lanes(square):
    return jnp.concatenate([square[k : k + 1, :] for k in range(8)], axis=1)


def to_square(lanes):
    return jnp.concatenate([lanes[:, 128 * k : 128 * k + 128] for k in range(8)], axis=0)


def own_first(square):
    swapped = jnp.concatenate([square[4:, :], square[:4, :]], axis=0)
    return jnp.where(lax.axis_index("core") == 0, square, swapped)


def lse2(parts):
    top = jnp.max(parts, axis=0)
    return top + jnp.log2(jnp.sum(jnp.exp2(parts - top[None]), axis=0))


def send(out_ref, square):
    out_ref[...] = jnp.broadcast_to(square[None], (16, 8, 128))


def terms(lanes):
    high = lanes.astype(jnp.bfloat16)
    rest = lanes - high.astype(jnp.float32)
    low = rest.astype(jnp.bfloat16)
    zeros = jnp.zeros((14, ROWS), jnp.bfloat16)
    return jnp.concatenate([high, low, zeros], axis=0)


def down(row):
    return jnp.transpose(jnp.broadcast_to(row, (128, 128)))[:, :1]


def across(column):
    return jnp.transpose(jnp.broadcast_to(column, (128, 128)))[:1, :]


def square_sums(block):
    wide = block.astype(jnp.float32)
    return jnp.sum(wide * wide, axis=1, keepdims=True)


def scores_kernel(data_ref, own_ref, far_ref, score_ref, out_ref, other_ref, sem):
    scale = LOG2E / EPSILON
    load = pltpu.make_async_copy(far_ref, other_ref, sem)
    load.start()
    data_norms = jnp.concatenate(
        [square_sums(data_ref[pl.ds(128 * k, 128), :]) for k in range(8)], axis=0
    )
    rows = []
    for k in range(4):
        if k == 2:
            load.wait()
        source = own_ref if k < 2 else other_ref
        noise = source[pl.ds(256 * (k % 2), 256), :]
        noise_norms = jnp.concatenate(
            [across(square_sums(noise[:128])), across(square_sums(noise[128:]))], axis=1
        )
        products = lax.dot_general(
            data_ref[...], noise, (((1,), (1,)), ((), ())), preferred_element_type=jnp.float32
        )
        scores = (2.0 * products - (data_norms + noise_norms)) * scale
        score_ref[:, pl.ds(256 * k, 256)] = scores
        top = jnp.max(scores, axis=0, keepdims=True)
        total = jnp.sum(jnp.exp2(scores - top), axis=0, keepdims=True)
        rows.append(top + jnp.log2(total))
    send(out_ref, own_first(to_square(jnp.concatenate(rows, axis=1))))


def columns_kernel(score_ref, in_ref, dual_ref, out_ref):
    dual = own_first(LOG2_MASS - lse2(in_ref[...]))
    dual_ref[...] = dual
    along = to_lanes(dual)
    rows = []
    for k in range(8):
        shifted = score_ref[pl.ds(128 * k, 128), :] + along
        top = jnp.max(shifted, axis=1, keepdims=True)
        total = jnp.sum(jnp.exp2(shifted - top), axis=1, keepdims=True)
        rows.append(across(top + jnp.log2(total)))
    send(out_ref, jnp.concatenate(rows, axis=0))


def plan_kernel(score_ref, dual_ref, in_ref, plan_ref, out_ref):
    along = to_lanes(dual_ref[...])
    dual = LOG2_MASS - lse2(in_ref[...])
    sums = jnp.zeros((1, ROWS), jnp.float32)
    for k in range(8):
        part = pl.ds(128 * k, 128)
        lifted = down(dual[k : k + 1, :] - LOG2_MASS)
        plan = jnp.exp2(score_ref[part, :] + along + lifted)
        plan_ref[part, :] = plan.astype(jnp.bfloat16)
        sums = sums + jnp.sum(plan, axis=0, keepdims=True)
    send(out_ref, own_first(to_square(sums)))


def column_sums_kernel(plan_ref, in_ref, out_ref):
    scale = own_first(1.0 / jnp.sum(in_ref[...], axis=0))
    sums = lax.dot_general(
        terms(to_lanes(scale)),
        plan_ref[...],
        (((1,), (1,)), ((), ())),
        preferred_element_type=jnp.float32,
    )
    send(out_ref, to_square(sums[0:1, :] + sums[1:2, :]))


def row_sums_kernel(plan_ref, in_ref, out_ref):
    scale = 1.0 / jnp.sum(in_ref[...], axis=0)
    sums = jnp.dot(terms(to_lanes(scale)), plan_ref[...], preferred_element_type=jnp.float32)
    send(out_ref, own_first(to_square(sums[0:1, :] + sums[1:2, :])))


def copies_kernel(data_ref, out_ref, sems):
    writes = [pltpu.make_async_copy(data_ref, out_ref.at[k], sems.at[k]) for k in range(16)]
    for write in writes:
        write.start()
    for write in writes:
        write.wait()


def tile_kernel(shard_ref, *refs):
    sources, (out_ref, sems) = refs[:7], refs[7:]
    loads = [
        pltpu.make_async_copy(source, out_ref.at[chip_rows(steps), :], sems.at[k])
        for k, (source, steps) in enumerate(zip((shard_ref, *sources), (0, *FOUND)))
    ]
    for load in loads:
        load.start()
    for load in loads:
        load.wait()


def with_total(body, total):
    high = total.astype(jnp.bfloat16).astype(jnp.float32)
    first = lax.broadcasted_iota(jnp.int32, total.shape, 1) < 64
    tail = jnp.where(first, high, total - high)
    return jnp.concatenate([body.astype(jnp.bfloat16), tail.astype(jnp.bfloat16)], axis=1)


def body_total(sent):
    tail = sent[:, WIDTH:].astype(jnp.float32)
    return sent[:, :WIDTH].astype(jnp.float32), tail + pltpu.roll(tail, 64, 1)


def summed(a, b):
    (body_a, total_a), (body_b, total_b) = body_total(a), body_total(b)
    return with_total(body_a + body_b, total_a + total_b)


def half_targets(weight_ref, data_ref, start, out_ref):
    ones = jnp.ones((ROWS, 128), jnp.bfloat16)
    for k in range(2):
        weights = weight_ref[:, pl.ds(start + 256 * k, 256)]
        found = [
            lax.dot_general(weights, side, (((0,), (0,)), ((), ())), preferred_element_type=jnp.float32)
            for side in (data_ref[...], ones)
        ]
        out_ref[pl.ds(256 * k, 256), :] = with_total(*found)


def other_targets_kernel(plan_ref, in_ref, data_ref, weight_ref, out_ref):
    scale = 1.0 / jnp.sum(in_ref[...], axis=0)
    for k in range(8):
        part = pl.ds(128 * k, 128)
        weights = plan_ref[part, :].astype(jnp.float32) * down(scale[k : k + 1, :])
        weight_ref[part, :] = weights.astype(jnp.bfloat16)
    half_targets(weight_ref, data_ref, ROWS // 2, out_ref)


def own_targets_kernel(weight_ref, data_ref, out_ref):
    half_targets(weight_ref, data_ref, 0, out_ref)


def piece(ref, offset):
    at = jnp.bitwise_and(lax.axis_index("z") + offset, 7)
    return ref[pl.ds(pl.multiple_of(at * PIECE, PIECE), PIECE), :]


def start_kernel(own_ref, got_ref, right_ref, left_ref, right2_ref, left2_ref):
    right_ref[...] = summed(piece(own_ref, 3), piece(got_ref, 3))
    left_ref[...] = summed(piece(own_ref, 5), piece(got_ref, 5))
    far = summed(piece(own_ref, 4), piece(got_ref, 4))
    right2_ref[...] = far[: PIECE // 2]
    left2_ref[...] = far[PIECE // 2 :]


def cores_kernel(own_ref, got_ref, out_ref):
    for k, steps in enumerate(LATE):
        out_ref[pl.ds(PIECE * k, PIECE), :] = summed(piece(own_ref, steps), piece(got_ref, steps))


LATE = (0, 1, 2, 6, 7)


def later(ref, steps):
    return ref[pl.ds(PIECE * LATE.index(steps), PIECE), :]


def join_kernel(offset, start, own_ref, got_ref, far_ref, out_ref):
    found = summed(later(own_ref, offset), got_ref[...])
    halves = [found[: PIECE // 2], found[PIECE // 2 :]]
    halves[start] = summed(halves[start], far_ref[...])
    out_ref[...] = jnp.concatenate(halves, axis=0)


def pass_kernel(offset, own_ref, got_ref, out_ref):
    out_ref[...] = summed(later(own_ref, offset), got_ref[...])


def velocity_kernel(own_ref, right_ref, left_ref, noise_ref, out_ref):
    found = [body_total(a) for a in (later(own_ref, 0), right_ref[...], left_ref[...])]
    body, total = (sum(values) for values in zip(*found))
    target = body / total[:, :1]
    out_ref[...] = (target - noise_ref[...].astype(jnp.float32)).astype(jnp.bfloat16)


SQUARE = jax.ShapeDtypeStruct((8, 128), jnp.float32)
COPIES = jax.ShapeDtypeStruct((16, 8, 128), jnp.float32)


def in_vmem(rows, dtype):
    return pltpu.VMEM((rows, 1024), dtype)


def run(kernel, outs, *args, flops=0, scratch=(), out_space=pltpu.VMEM, in_hbm=()):
    spaces = [pltpu.HBM if k in in_hbm else pltpu.VMEM for k in range(len(args))]
    return pl.pallas_call(
        kernel,
        out_shape=outs,
        in_specs=[pl.BlockSpec(memory_space=space) for space in spaces],
        out_specs=jax.tree.map(lambda _: pl.BlockSpec(memory_space=out_space), outs),
        scratch_shapes=scratch,
        compiler_params=pltpu.CompilerParams(vmem_limit_bytes=40 * 1024 * 1024),
        cost_estimate=pl.CostEstimate(flops=flops, bytes_accessed=4 << 20, transcendentals=0),
    )(*args)


def keep(a):
    return pltpu.with_memory_space_constraint(a, pltpu.VMEM)


def sent_rows(count):
    return pltpu.VMEM((count, SENT), jnp.bfloat16)


def per_device(noise_latents, data_latents):
    copies = run(
        copies_kernel,
        pltpu.HBM((16, PIECE, WIDTH), jnp.bfloat16),
        data_latents,
        scratch=[pltpu.SemaphoreType.DMA((16,))],
        out_space=pltpu.HBM,
        in_hbm=(0,),
    )
    columns = keep(spread(copies, COL_GROUP).reshape(ROWS, WIDTH))
    found = lax.cond(
        lax.axis_index("x") < 4, gather_z, lambda shard: (jnp.zeros_like(shard),) * 7, noise_latents
    )
    own_rows = run(
        tile_kernel,
        in_vmem(ROWS // 2, jnp.bfloat16),
        noise_latents,
        *found,
        scratch=[pltpu.SemaphoreType.DMA((8,))],
        in_hbm=range(8),
    )
    other_rows = pltpu.with_memory_space_constraint(swap_core(own_rows), pltpu.HBM)

    scores, parts = run(
        scores_kernel,
        (in_vmem(ROWS, jnp.float32), COPIES),
        columns,
        keep(own_rows),
        other_rows,
        flops=2 * ROWS * ROWS * WIDTH,
        scratch=[pltpu.VMEM((ROWS // 2, WIDTH), jnp.bfloat16), pltpu.SemaphoreType.DMA],
        in_hbm=(2,),
    )
    scores = keep(scores)
    row_dual, parts = run(columns_kernel, (SQUARE, COPIES), scores, spread(parts, ROW_GROUP))
    plan, parts = run(
        plan_kernel,
        (in_vmem(ROWS, jnp.bfloat16), COPIES),
        scores,
        row_dual,
        spread(parts, COL_GROUP),
    )
    plan = keep(plan)
    parts = run(column_sums_kernel, COPIES, plan, spread(parts, ROW_GROUP))
    parts = run(row_sums_kernel, COPIES, plan, spread(parts, COL_GROUP))
    parts = run(column_sums_kernel, COPIES, plan, spread(parts, ROW_GROUP))
    weights, others = run(
        other_targets_kernel,
        (in_vmem(ROWS, jnp.bfloat16), sent_rows(ROWS // 2)),
        plan,
        spread(parts, COL_GROUP),
        columns,
        flops=ROWS * ROWS * WIDTH,
    )
    got = swap_core(others)
    own = run(
        own_targets_kernel,
        sent_rows(ROWS // 2),
        keep(weights),
        columns,
        flops=ROWS * ROWS * WIDTH,
    )
    own, got = keep(own), keep(got)
    right, left, right2, left2 = run(
        start_kernel,
        tuple(sent_rows(count) for count in (PIECE, PIECE, PIECE // 2, PIECE // 2)),
        own,
        got,
    )
    own = run(cores_kernel, sent_rows(PIECE * len(LATE)), own, got)
    own = keep(own)
    right, left = shift_z(right, 1), shift_z(left, -1)
    right2, left2 = shift_z(right2, 2), shift_z(left2, -2)
    joined = sent_rows(PIECE)
    right = shift_z(run(functools.partial(join_kernel, 2, 0), joined, own, keep(right), keep(right2)), 1)
    left = shift_z(run(functools.partial(join_kernel, 6, 1), joined, own, keep(left), keep(left2)), -1)
    right = shift_z(run(functools.partial(pass_kernel, 1), joined, own, keep(right)), 1)
    left = shift_z(run(functools.partial(pass_kernel, 7), joined, own, keep(left)), -1)
    velocity = jax.ShapeDtypeStruct((PIECE, WIDTH), jnp.bfloat16)
    return run(velocity_kernel, velocity, own, keep(right), keep(left), noise_latents)


def solution(mesh):
    fine = Mesh(mesh.devices.reshape(SIZES), AXES)
    rows = P(AXES, None)
    return jax.shard_map(
        per_device, mesh=fine, in_specs=(rows, rows), out_specs=rows, check_vma=False
    )
```

```python
import functools
import math

import jax
import jax.numpy as jnp
from jax import lax
from jax.experimental import pallas as pl
from jax.experimental.pallas import tpu as pltpu
from jax.sharding import Mesh
from jax.sharding import PartitionSpec as P

WIDTH = 1024
ROWS = 1024
PIECE = 64
SENT = WIDTH + 128
eps_factor = 0.3

AXES = ("x", "yh", "core", "yl", "z")
SIZES = (4, 2, 2, 2, 8)
ROW_GROUP = ("z", "core")
COL_GROUP = ("x", "yh", "yl")

EPSILON = eps_factor * math.sqrt(WIDTH)
LOG2E = math.log2(math.e)
LOG2_MASS = -math.log2(16384)


def device_pairs(move):
    pairs = []
    for x in range(4):
        for yh in range(2):
            for core in range(2):
                for yl in range(2):
                    for z in range(8):
                        place = (x, yh, core, yl, z)
                        pairs.append((number(place), number(move(*place))))
    return pairs


def number(place):
    index = 0
    for size, at in zip(SIZES, place):
        index = index * size + at % size
    return index


def shift_z(a, by):
    return lax.ppermute(a, AXES, device_pairs(lambda x, yh, c, yl, z: (x, yh, c, yl, z + by)))


def swap_core(a):
    return lax.ppermute(a, AXES, device_pairs(lambda x, yh, c, yl, z: (x, yh, 1 - c, yl, z)))


def spread(copies, group):
    return lax.all_to_all(copies, group, 0, 0)


def shift_out(a, by):
    return lax.ppermute(
        a, AXES, device_pairs(lambda x, yh, c, yl, z: (x, yh, c, yl, z + by * (1 - 2 * c)))
    )


def gather_z(shard):
    ahead, behind = shift_out(shard, 1), shift_out(shard, -1)
    ahead2, behind2 = shift_out(shard, 2), shift_out(shard, -2)
    far = shift_out(ahead2, 2)
    return ahead, behind, ahead2, behind2, shift_out(ahead2, 1), shift_out(behind2, -1), far


FOUND = (-1, 1, -2, 2, -3, 3, 4)


def chip_rows(steps):
    at = lax.axis_index("z") + steps * (1 - 2 * lax.axis_index("core"))
    return pl.ds(pl.multiple_of(jnp.bitwise_and(at, 7) * PIECE, PIECE), PIECE)


def to_lanes(square):
    return jnp.concatenate([square[k : k + 1, :] for k in range(8)], axis=1)


def to_square(lanes):
    return jnp.concatenate([lanes[:, 128 * k : 128 * k + 128] for k in range(8)], axis=0)


def own_first(square):
    swapped = jnp.concatenate([square[4:, :], square[:4, :]], axis=0)
    return jnp.where(lax.axis_index("core") == 0, square, swapped)


def lse2(parts):
    top = jnp.max(parts, axis=0)
    return top + jnp.log2(jnp.sum(jnp.exp2(parts - top[None]), axis=0))


def send(out_ref, square):
    out_ref[...] = jnp.broadcast_to(square[None], (16, 8, 128)).astype(out_ref.dtype)


def received(in_ref):
    return jnp.sum(in_ref[...].astype(jnp.float32), axis=0)


def terms(lanes):
    high = lanes.astype(jnp.bfloat16)
    rest = lanes - high.astype(jnp.float32)
    low = rest.astype(jnp.bfloat16)
    zeros = jnp.zeros((14, ROWS), jnp.bfloat16)
    return jnp.concatenate([high, low, zeros], axis=0)


def down(row):
    return jnp.transpose(jnp.broadcast_to(row, (128, 128)))[:, :1]


def across(column):
    return jnp.transpose(jnp.broadcast_to(column, (128, 128)))[:1, :]


def square_sums(block):
    wide = block.astype(jnp.float32)
    return jnp.sum(wide * wide, axis=1, keepdims=True)


def scores_kernel(data_ref, own_ref, far_ref, score_ref, out_ref, other_ref, sem):
    scale = LOG2E / EPSILON
    load = pltpu.make_async_copy(far_ref, other_ref, sem)
    load.start()
    data_norms = jnp.concatenate(
        [square_sums(data_ref[pl.ds(128 * k, 128), :]) for k in range(8)], axis=0
    )
    rows = []
    for k in range(4):
        if k == 2:
            load.wait()
        source = own_ref if k < 2 else other_ref
        noise = source[pl.ds(256 * (k % 2), 256), :]
        noise_norms = jnp.concatenate(
            [across(square_sums(noise[:128])), across(square_sums(noise[128:]))], axis=1
        )
        products = lax.dot_general(
            data_ref[...], noise, (((1,), (1,)), ((), ())), preferred_element_type=jnp.float32
        )
        scores = (2.0 * products - (data_norms + noise_norms)) * scale
        score_ref[:, pl.ds(256 * k, 256)] = scores
        top = jnp.max(scores, axis=0, keepdims=True)
        total = jnp.sum(jnp.exp2(scores - top), axis=0, keepdims=True)
        rows.append(top + jnp.log2(total))
    send(out_ref, own_first(to_square(jnp.concatenate(rows, axis=1))))


def columns_kernel(score_ref, in_ref, dual_ref, out_ref):
    dual = own_first(LOG2_MASS - lse2(in_ref[...]))
    dual_ref[...] = dual
    along = to_lanes(dual)
    rows = []
    for k in range(8):
        shifted = score_ref[pl.ds(128 * k, 128), :] + along
        top = jnp.max(shifted, axis=1, keepdims=True)
        total = jnp.sum(jnp.exp2(shifted - top), axis=1, keepdims=True)
        rows.append(across(top + jnp.log2(total)))
    send(out_ref, jnp.concatenate(rows, axis=0))


def plan_kernel(score_ref, dual_ref, in_ref, plan_ref, out_ref):
    along = to_lanes(dual_ref[...])
    dual = LOG2_MASS - lse2(in_ref[...])
    sums = jnp.zeros((1, ROWS), jnp.float32)
    for k in range(8):
        part = pl.ds(128 * k, 128)
        lifted = down(dual[k : k + 1, :] - LOG2_MASS)
        plan = jnp.exp2(score_ref[part, :] + along + lifted)
        plan_ref[part, :] = plan.astype(jnp.bfloat16)
        sums = sums + jnp.sum(plan, axis=0, keepdims=True)
    send(out_ref, own_first(to_square(sums)))


def column_sums_kernel(plan_ref, in_ref, out_ref):
    scale = own_first(1.0 / received(in_ref))
    sums = lax.dot_general(
        terms(to_lanes(scale)),
        plan_ref[...],
        (((1,), (1,)), ((), ())),
        preferred_element_type=jnp.float32,
    )
    send(out_ref, to_square(sums[0:1, :] + sums[1:2, :]))


def row_sums_kernel(plan_ref, in_ref, out_ref):
    scale = 1.0 / received(in_ref)
    sums = jnp.dot(terms(to_lanes(scale)), plan_ref[...], preferred_element_type=jnp.float32)
    send(out_ref, own_first(to_square(sums[0:1, :] + sums[1:2, :])))


def copies_kernel(data_ref, out_ref, sems):
    writes = [pltpu.make_async_copy(data_ref, out_ref.at[k], sems.at[k]) for k in range(16)]
    for write in writes:
        write.start()
    for write in writes:
        write.wait()


def tile_kernel(shard_ref, *refs):
    sources, (out_ref, sems) = refs[:7], refs[7:]
    loads = [
        pltpu.make_async_copy(source, out_ref.at[chip_rows(steps), :], sems.at[k])
        for k, (source, steps) in enumerate(zip((shard_ref, *sources), (0, *FOUND)))
    ]
    for load in loads:
        load.start()
    for load in loads:
        load.wait()


def with_total(body, total):
    high = total.astype(jnp.bfloat16).astype(jnp.float32)
    first = lax.broadcasted_iota(jnp.int32, total.shape, 1) < 64
    tail = jnp.where(first, high, total - high)
    return jnp.concatenate([body.astype(jnp.bfloat16), tail.astype(jnp.bfloat16)], axis=1)


def body_total(sent):
    tail = sent[:, WIDTH:].astype(jnp.float32)
    return sent[:, :WIDTH].astype(jnp.float32), tail + pltpu.roll(tail, 64, 1)


def summed(a, b):
    (body_a, total_a), (body_b, total_b) = body_total(a), body_total(b)
    return with_total(body_a + body_b, total_a + total_b)


def half_targets(weight_ref, data_ref, start, out_ref):
    ones = jnp.ones((ROWS, 128), jnp.bfloat16)
    for k in range(2):
        weights = weight_ref[:, pl.ds(start + 256 * k, 256)]
        found = [
            lax.dot_general(weights, side, (((0,), (0,)), ((), ())), preferred_element_type=jnp.float32)
            for side in (data_ref[...], ones)
        ]
        out_ref[pl.ds(256 * k, 256), :] = with_total(*found)


def other_targets_kernel(plan_ref, in_ref, data_ref, weight_ref, out_ref):
    scale = 1.0 / received(in_ref)
    for k in range(8):
        part = pl.ds(128 * k, 128)
        weights = plan_ref[part, :].astype(jnp.float32) * down(scale[k : k + 1, :])
        weight_ref[part, :] = weights.astype(jnp.bfloat16)
    half_targets(weight_ref, data_ref, ROWS // 2, out_ref)


def own_targets_kernel(weight_ref, data_ref, out_ref):
    half_targets(weight_ref, data_ref, 0, out_ref)


def piece(ref, offset):
    at = jnp.bitwise_and(lax.axis_index("z") + offset, 7)
    return ref[pl.ds(pl.multiple_of(at * PIECE, PIECE), PIECE), :]


def start_kernel(own_ref, got_ref, right_ref, left_ref, right2_ref, left2_ref):
    right_ref[...] = summed(piece(own_ref, 3), piece(got_ref, 3))
    left_ref[...] = summed(piece(own_ref, 5), piece(got_ref, 5))
    far = summed(piece(own_ref, 4), piece(got_ref, 4))
    right2_ref[...] = far[: PIECE // 2]
    left2_ref[...] = far[PIECE // 2 :]


def cores_kernel(own_ref, got_ref, out_ref):
    for k, steps in enumerate(LATE):
        out_ref[pl.ds(PIECE * k, PIECE), :] = summed(piece(own_ref, steps), piece(got_ref, steps))


LATE = (0, 1, 2, 6, 7)


def later(ref, steps):
    return ref[pl.ds(PIECE * LATE.index(steps), PIECE), :]


def join_kernel(offset, start, own_ref, got_ref, far_ref, out_ref):
    found = summed(later(own_ref, offset), got_ref[...])
    halves = [found[: PIECE // 2], found[PIECE // 2 :]]
    halves[start] = summed(halves[start], far_ref[...])
    out_ref[...] = jnp.concatenate(halves, axis=0)


def pass_kernel(offset, own_ref, got_ref, out_ref):
    out_ref[...] = summed(later(own_ref, offset), got_ref[...])


def velocity_kernel(own_ref, right_ref, left_ref, noise_ref, out_ref):
    found = [body_total(a) for a in (later(own_ref, 0), right_ref[...], left_ref[...])]
    body, total = (sum(values) for values in zip(*found))
    target = body / total[:, :1]
    out_ref[...] = (target - noise_ref[...].astype(jnp.float32)).astype(jnp.bfloat16)


SQUARE = jax.ShapeDtypeStruct((8, 128), jnp.float32)
COPIES = jax.ShapeDtypeStruct((16, 8, 128), jnp.float32)
SUMS = jax.ShapeDtypeStruct((16, 8, 128), jnp.bfloat16)


def in_vmem(rows, dtype):
    return pltpu.VMEM((rows, 1024), dtype)


def run(kernel, outs, *args, flops=0, scratch=(), out_space=pltpu.VMEM, in_hbm=()):
    spaces = [pltpu.HBM if k in in_hbm else pltpu.VMEM for k in range(len(args))]
    return pl.pallas_call(
        kernel,
        out_shape=outs,
        in_specs=[pl.BlockSpec(memory_space=space) for space in spaces],
        out_specs=jax.tree.map(lambda _: pl.BlockSpec(memory_space=out_space), outs),
        scratch_shapes=scratch,
        compiler_params=pltpu.CompilerParams(vmem_limit_bytes=40 * 1024 * 1024),
        cost_estimate=pl.CostEstimate(flops=flops, bytes_accessed=4 << 20, transcendentals=0),
    )(*args)


def keep(a):
    return pltpu.with_memory_space_constraint(a, pltpu.VMEM)


def sent_rows(count):
    return pltpu.VMEM((count, SENT), jnp.bfloat16)


def per_device(noise_latents, data_latents):
    copies = run(
        copies_kernel,
        pltpu.HBM((16, PIECE, WIDTH), jnp.bfloat16),
        data_latents,
        scratch=[pltpu.SemaphoreType.DMA((16,))],
        out_space=pltpu.HBM,
        in_hbm=(0,),
    )
    columns = keep(spread(copies, COL_GROUP).reshape(ROWS, WIDTH))
    found = lax.cond(
        lax.axis_index("x") < 4, gather_z, lambda shard: (jnp.zeros_like(shard),) * 7, noise_latents
    )
    own_rows = run(
        tile_kernel,
        in_vmem(ROWS // 2, jnp.bfloat16),
        noise_latents,
        *found,
        scratch=[pltpu.SemaphoreType.DMA((8,))],
        in_hbm=range(8),
    )
    other_rows = pltpu.with_memory_space_constraint(swap_core(own_rows), pltpu.HBM)

    scores, parts = run(
        scores_kernel,
        (in_vmem(ROWS, jnp.float32), COPIES),
        columns,
        keep(own_rows),
        other_rows,
        flops=2 * ROWS * ROWS * WIDTH,
        scratch=[pltpu.VMEM((ROWS // 2, WIDTH), jnp.bfloat16), pltpu.SemaphoreType.DMA],
        in_hbm=(2,),
    )
    scores = keep(scores)
    row_dual, parts = run(columns_kernel, (SQUARE, COPIES), scores, spread(parts, ROW_GROUP))
    plan, parts = run(
        plan_kernel,
        (in_vmem(ROWS, jnp.bfloat16), SUMS),
        scores,
        row_dual,
        spread(parts, COL_GROUP),
    )
    plan = keep(plan)
    parts = run(column_sums_kernel, SUMS, plan, spread(parts, ROW_GROUP))
    parts = run(row_sums_kernel, SUMS, plan, spread(parts, COL_GROUP))
    parts = run(column_sums_kernel, SUMS, plan, spread(parts, ROW_GROUP))
    weights, others = run(
        other_targets_kernel,
        (in_vmem(ROWS, jnp.bfloat16), sent_rows(ROWS // 2)),
        plan,
        spread(parts, COL_GROUP),
        columns,
        flops=ROWS * ROWS * WIDTH,
    )
    got = swap_core(others)
    own = run(
        own_targets_kernel,
        sent_rows(ROWS // 2),
        keep(weights),
        columns,
        flops=ROWS * ROWS * WIDTH,
    )
    own, got = keep(own), keep(got)
    right, left, right2, left2 = run(
        start_kernel,
        tuple(sent_rows(count) for count in (PIECE, PIECE, PIECE // 2, PIECE // 2)),
        own,
        got,
    )
    own = run(cores_kernel, sent_rows(PIECE * len(LATE)), own, got)
    own = keep(own)
    right, left = shift_z(right, 1), shift_z(left, -1)
    right2, left2 = shift_z(right2, 2), shift_z(left2, -2)
    joined = sent_rows(PIECE)
    right = shift_z(run(functools.partial(join_kernel, 2, 0), joined, own, keep(right), keep(right2)), 1)
    left = shift_z(run(functools.partial(join_kernel, 6, 1), joined, own, keep(left), keep(left2)), -1)
    right = shift_z(run(functools.partial(pass_kernel, 1), joined, own, keep(right)), 1)
    left = shift_z(run(functools.partial(pass_kernel, 7), joined, own, keep(left)), -1)
    velocity = jax.ShapeDtypeStruct((PIECE, WIDTH), jnp.bfloat16)
    return run(velocity_kernel, velocity, own, keep(right), keep(left), noise_latents)


def solution(mesh):
    fine = Mesh(mesh.devices.reshape(SIZES), AXES)
    rows = P(AXES, None)
    return jax.shard_map(
        per_device, mesh=fine, in_specs=(rows, rows), out_specs=rows, check_vma=False
    )
```
